32 devices in a mesh: alpha: 8 (over z, x), beta: 4 (over y, core).
Axes of the slice: x: 2, y: 2, z: 4, core: 2. Of those that a mesh axis runs over, the one named last changes fastest.
Arguments:
- coeffs: float32 [6144, 6144], P('alpha', 'beta'), may hold values from -6 to 6
- denominator: float32 [6144, 6144], P('alpha', 'beta'), may hold values from 1.5 to 6
- coupling: bfloat16 [6144, 4, 768], P('alpha'), may hold values from -0.15625 to 0.15625
- tile_cols: int32 [8, 4], replicated, may hold values from 0 to 7, as said below
- tile_count: int32 [8], replicated, may hold values from 1 to 4, as said below
Outputs:
- coeffs_out: float32 [6144, 6144], P('alpha', 'beta')
The draws below stay inside these ranges and needn't reach their ends.
Inputs may be any that keep to these rules, and one draw needn't show every extreme that they name: `tile_cols`: in every row the 4 entries are distinct; only the first tile_count entries of a row name coupled tiles, the others are unused. `tile_count`: some tile row has exactly 4 coupled tiles.
All inputs are finite; a program needn't handle non-finite values.
Results may differ from the reference program's by a relative error of at most 0.0017.
Values may be sent and summed in bfloat16 or wider, within the bound.
No kernel may reach another device: no remote copies, remote signals or barrier semaphores. Data moves between devices by JAX's collectives and lax.ppermute only.
A program may use at most 128 MiB of HBM per device.

```python
import math
import jax
import jax.numpy as jnp
from jax import lax

N = 6144
TILE = 768
MAXT = 4
STEPS = 2
NT = 8


def tile_plan(key):
    base = jax.random.fold_in(key, 7741)
    row_keys = jax.random.split(jax.random.fold_in(base, 1), NT)
    columns = jax.vmap(lambda row_key: jax.random.permutation(row_key, NT)[:MAXT])(row_keys)
    filled = jax.random.randint(jax.random.fold_in(base, 2), (NT,), 1, 3)
    busiest = jax.random.randint(jax.random.fold_in(base, 3), (), 0, NT)
    filled = jnp.where(jnp.arange(NT) == busiest, MAXT, filled)
    return (columns.astype(jnp.int32), filled.astype(jnp.int32))


def draw_tile_cols(key, part):
    return tile_plan(key)[0]


def draw_tile_count(key, part):
    return tile_plan(key)[1]


def block_scale(rng, extent, cuts, smallest, high):
    def one(dim, blocks):
        heights = jax.random.uniform(jax.random.fold_in(jax.random.fold_in(rng, 6), dim), (blocks,), jnp.float32, smallest / len(cuts), high / len(cuts))
        return jnp.repeat(jnp.exp(heights), extent[dim] // blocks).reshape((-1,) + (1,) * (len(extent) - dim - 1))

    loudness = one(*cuts[0])
    for cut in cuts[1:]:
        loudness = loudness * one(*cut)
    return loudness


def bell_draw(stream_key, dims, spread, limit, cuts=(), kind=jnp.bfloat16):
    array = spread * jax.random.normal(stream_key, dims, jnp.float32)
    if cuts:
        array = array * block_scale(stream_key, dims, cuts, -0.22, 0.18)
    return jnp.clip(array, -limit, limit).astype(kind)


def setup_inputs(seed: int = 0) -> dict:
    key_list = jax.random.split(jax.random.key(seed), 6)
    return {
        "coeffs": bell_draw(key_list[0], (N, N), 1.0, 6.0, ((0, 8), (1, 4)), jnp.float32),
        "denominator": jnp.clip(jnp.exp(math.log(6.0) - 1.3862944 * jax.random.uniform(key_list[1], (N, N), jnp.float32) ** block_scale(key_list[1], (N, N), ((0, 8), (1, 4)), -0.2, 0.2)), 1.5, 6.0),
        "coupling": bell_draw(key_list[2], (N, MAXT, TILE), (2 * TILE) ** -0.5, 0.15625, ((0, 8),)),
        "tile_cols": draw_tile_cols(jax.random.fold_in(key_list[5], 71), 0),
        "tile_count": draw_tile_count(jax.random.fold_in(key_list[5], 71), 0),
    }


def sigma_whole(coeffs, coupling, tile_cols, tile_count):
    coeff_half = coeffs.astype(jnp.bfloat16)

    def row_block(tile_row):
        row_tiles = lax.dynamic_slice_in_dim(coupling, (tile_row * TILE).astype(jnp.int32), TILE, 0)

        def add_slot(slot, running):
            column = tile_cols[tile_row, slot].astype(jnp.int32)
            column_block = lax.dynamic_slice_in_dim(coeff_half, (column * TILE).astype(jnp.int32), TILE, 0)
            weights = lax.dynamic_index_in_dim(row_tiles, slot, 1, keepdims=False)
            return running + jnp.dot(weights, column_block, preferred_element_type=jnp.float32)

        return lax.fori_loop(jnp.int32(0), tile_count[tile_row].astype(jnp.int32), add_slot,
                             jnp.zeros((TILE, N), jnp.float32))

    blocks = lax.map(row_block, jnp.arange(NT, dtype=jnp.int32))
    return blocks.reshape(N, N)


def reference(coeffs, denominator, coupling, tile_cols, tile_count):
    current = coeffs
    for step_index in range(STEPS):
        sigma = sigma_whole(current, coupling, tile_cols, tile_count)
        current = current - (sigma + sigma.T) / denominator
    return current
```

```python
import jax
import jax.numpy as jnp
from jax import lax
from jax.experimental import pallas as pl
from jax.experimental.pallas import tpu as pltpu
from jax.sharding import PartitionSpec as P

STEPS = 2
COUPLING_MAX = 0.15625
DENOMINATOR_MIN = 1.5
HALF_TOP = 60000.0
AXES = ("alpha", "beta")
ROW_CHUNKS = 2


class Grid:
    def __init__(self, alpha_devices, beta_devices):
        self.bands = beta_devices
        self.lanes = alpha_devices // beta_devices
        self.per_lane = beta_devices // self.lanes

    def index(self, band, lane, beta):
        return (band * self.lanes + lane) * self.bands + beta

    def send(self, value, where):
        pairs = []
        for band in range(self.bands):
            for lane in range(self.lanes):
                for beta in range(self.bands):
                    target = where(band, lane, beta)
                    if target is not None:
                        pairs.append((self.index(band, lane, beta), self.index(*target)))
        if all(source == target for source, target in pairs):
            return value
        return lax.ppermute(value, AXES, pairs)


def gather_couplings(grid, coupling, band, beta):
    rows, slots, _ = coupling.shape
    bands = grid.bands
    chunk = rows // bands
    own = lax.dynamic_slice_in_dim(coupling, beta * chunk, chunk, 0)
    gathered = []
    for slot in range(slots):
        upward, downward = [own[:, slot]], [own[:, slot]]
        for _ in range(bands - 1):
            upward.append(grid.send(upward[-1], lambda z, x, b: (z + 1, x, b) if z + 1 < bands else None))
            downward.append(grid.send(downward[-1], lambda z, x, b: (z - 1, x, b) if z > 0 else None))
        line = [upward[0]] + [jnp.where(band >= hop, upward[hop], downward[bands - hop]) for hop in range(1, bands)]
        pieces = {0: jnp.stack(line)}
        bit = bands // 2
        while bit:
            received = {
                key ^ bit: grid.send(piece, lambda z, x, b, bit=bit: (z, x, b ^ bit)) for key, piece in pieces.items()
            }
            pieces.update(received)
            bit //= 2
        pieces = [pieces[key] for key in range(bands)]
        if chunk % 16:
            whole = jnp.take(jnp.stack(pieces), beta ^ jnp.arange(bands), axis=0)
            pieces = [whole.transpose(1, 0, 2, 3).reshape(bands, rows, whole.shape[3])]
        gathered.append(pieces)
    return gathered


def to_columns(grid, half, band, lane, beta):
    rows, cols = half.shape
    bands, lanes = grid.bands, grid.lanes
    strip = cols // bands
    part = rows // ROW_CHUNKS
    whole = jnp.zeros((bands, lanes, rows, strip), half.dtype)
    for chunk in range(ROW_CHUNKS):
        block = half[chunk * part : (chunk + 1) * part]
        first = []
        for key in range(bands):
            piece = lax.dynamic_slice(block, (0, (beta ^ key) * strip), (part, strip))
            first.append(grid.send(piece, lambda z, x, b: (z, x, b ^ key)))
        first = jnp.stack(first)
        for key in range(bands):
            piece = lax.dynamic_index_in_dim(first, band ^ key ^ beta, 0, keepdims=False)
            piece = grid.send(piece, lambda z, x, b: (z ^ key, x, b))
            for turn in range(lanes):
                other = grid.send(piece, lambda z, x, b: (z, (x + turn) % lanes, b))
                place = (band ^ key, (lane - turn) % lanes, chunk * part, 0)
                whole = lax.dynamic_update_slice(whole, other[None, None], place)
    return whole.reshape(bands * lanes * rows, strip)


def product_kernel(slots, pieces, hop_ref, column_ref, count_ref, offset_ref, *refs):
    block = pl.program_id(0)
    coeff_ref, out_ref = refs[slots * pieces], refs[slots * pieces + 1]
    chunk, tile = refs[0].shape[1:]
    for piece in range(pieces):
        place = pl.ds(pl.multiple_of(offset_ref[piece], chunk), chunk)
        for slot in range(slots):

            def product():
                first = pl.multiple_of(column_ref[block * slots + slot] * tile, tile)
                return jnp.dot(
                    refs[slot * pieces + piece][0], coeff_ref[pl.ds(first, tile), :], preferred_element_type=jnp.float32
                )

            if slot == 0:
                out_ref[0, place, :] = product()
            else:

                @pl.when(slot < count_ref[block])
                def _():
                    out_ref[0, place, :] += product()


def products(couplings, columns, hops, tile_columns, counts, offsets):
    slots, pieces = len(couplings), len(couplings[0])
    bands, chunk, tile = couplings[0][0].shape
    strip = columns.shape[1]
    spec = pl.BlockSpec((1, chunk, tile), lambda i, hop, *_: (hop[i], 0, 0))
    return pl.pallas_call(
        lambda *refs: product_kernel(slots, pieces, *refs),
        grid_spec=pltpu.PrefetchScalarGridSpec(
            num_scalar_prefetch=4,
            grid=(bands,),
            in_specs=[spec] * (slots * pieces) + [pl.BlockSpec(columns.shape, lambda i, *_: (0, 0))],
            out_specs=pl.BlockSpec((1, pieces * chunk, strip), lambda i, *_: (i, 0, 0)),
        ),
        out_shape=jax.ShapeDtypeStruct((bands, pieces * chunk, strip), jnp.float32),
        compiler_params=pltpu.CompilerParams(vmem_limit_bytes=48 << 20),
        cost_estimate=pl.CostEstimate(
            flops=2 * bands * slots * pieces * chunk * tile * strip,
            bytes_accessed=2 * bands * slots * pieces * chunk * tile,
            transcendentals=0,
        ),
    )(hops, tile_columns, counts, offsets, *[piece for slot in couplings for piece in slot], columns)


def bring_home(grid, sigma, scale, band, lane, beta):
    bands, rows, strip = sigma.shape
    lanes, per_lane = grid.lanes, grid.per_lane
    scaled = (sigma * scale).astype(jnp.float16)
    mirrored = scaled.transpose(0, 2, 1)
    direct = jnp.zeros((rows, bands * strip), jnp.float16)
    mirror = jnp.zeros((rows, bands * strip), jnp.float16)
    for key in range(bands):
        piece = lax.dynamic_index_in_dim(scaled, beta ^ key, 0, keepdims=False)
        piece = grid.send(piece, lambda z, x, b: (b ^ key, x, z))
        direct = lax.dynamic_update_slice(direct, piece, (0, (band ^ key) * strip))
    for key in range(bands):
        target = (lane * per_lane + beta % per_lane) ^ key
        piece = lax.dynamic_index_in_dim(mirrored, target, 0, keepdims=False)
        piece = grid.send(piece, lambda z, x, b: (z, b // per_lane, (x * per_lane + b % per_lane) ^ key))
        source = beta ^ key
        mirror = lax.dynamic_update_slice(mirror, piece, ((source % per_lane) * strip, (source // per_lane) * rows))
    return direct, mirror


def body(coeffs, denominator, coupling, tile_cols, tile_count):
    rows = coeffs.shape[0]
    _, slots, tile = coupling.shape
    grid = Grid(lax.axis_size("alpha"), lax.axis_size("beta"))
    alpha, beta = lax.axis_index("alpha"), lax.axis_index("beta")
    band, lane = alpha // grid.lanes, alpha % grid.lanes
    every = jnp.arange(grid.bands, dtype=jnp.int32)
    tile_rows = (every * grid.lanes + lane) * rows // tile
    tile_columns = jnp.take(tile_cols, tile_rows, axis=0).reshape(-1)
    counts = jnp.take(tile_count, tile_rows)
    hops = (band - every) % grid.bands
    couplings = gather_couplings(grid, coupling, band, beta)
    pieces = len(couplings[0])
    offsets = (beta ^ every) * (rows // grid.bands) if pieces > 1 else jnp.zeros((1,), jnp.int32)

    growth = slots * tile * COUPLING_MAX
    largest = jnp.maximum(lax.pmax(jnp.max(jnp.abs(coeffs)), AXES), 1e-30)
    current = coeffs
    for step_index in range(STEPS):
        scale = HALF_TOP / (growth * largest)
        largest = largest * (1 + 2 * growth / DENOMINATOR_MIN)
        columns = to_columns(grid, current.astype(jnp.bfloat16), band, lane, beta)
        sigma = products(couplings, columns, hops, tile_columns, counts, offsets)
        direct, mirror = bring_home(grid, sigma, scale, band, lane, beta)
        total = (direct.astype(jnp.float32) + mirror.astype(jnp.float32)) / scale
        current = current - total / denominator
    return current


def solution(mesh):
    placed = (P("alpha", "beta"), P("alpha", "beta"), P("alpha", None, None), P(), P())
    return jax.shard_map(
        body, mesh=mesh, in_specs=placed, out_specs=P("alpha", "beta"), check_vma=False
    )
```

```python
import jax
import jax.numpy as jnp
from jax import lax
from jax.experimental import pallas as pl
from jax.experimental.pallas import tpu as pltpu
from jax.sharding import PartitionSpec as P

STEPS = 2
COUPLING_MAX = 0.15625
DENOMINATOR_MIN = 1.5
HALF_TOP = 60000.0
AXES = ("alpha", "beta")
ROW_CHUNKS = 3


class Grid:
    def __init__(self, alpha_devices, beta_devices):
        self.bands = beta_devices
        self.lanes = alpha_devices // beta_devices
        self.majors = beta_devices // 2
        self.per_lane = self.majors // self.lanes
        self.places = [
            (band, lane, major, minor)
            for band in range(self.bands)
            for lane in range(self.lanes)
            for major in range(self.majors)
            for minor in range(2)
        ]

    def index(self, band, lane, major, minor):
        return ((band * self.lanes + lane) * self.majors + major) * 2 + minor

    def send(self, value, where):
        pairs = [(self.index(*place), self.index(*where(*place))) for place in self.places]
        if all(source == target for source, target in pairs):
            return value
        return lax.ppermute(value, AXES, pairs)


def largest_anywhere(grid, value):
    devices = len(grid.places)
    largest = jnp.full((8, 128), value)
    bit = 1
    while bit < devices:
        pairs = [(device, device ^ bit) for device in range(devices)]
        largest = jnp.maximum(largest, lax.ppermute(largest, AXES, pairs))
        bit *= 2
    return largest[0, 0]


def gather_bands(grid, own, band):
    held = own[None]
    order = [[z] for z in range(grid.bands)]
    width = 2
    while width <= grid.bands:
        half = width // 2
        moving = held
        origin = list(range(grid.bands))
        kept, kept_origin = None, [None] * grid.bands
        for hop in range(half):
            partner = list(range(grid.bands))
            for base in range(0, grid.bands, width):
                low, high = base + half - 1, base + half
                if hop == 0:
                    pairs = [(low, high)]
                else:
                    pairs = [(low - hop + 1, low - hop), (high + hop - 1, high + hop)]
                for one, other in pairs:
                    partner[one], partner[other] = other, one
            moving = grid.send(moving, lambda z, x, m, n: (partner[z], x, m, n))
            origin = [origin[partner[z]] for z in range(grid.bands)]
            takes = [(half - 1 - z % width if z % width < half else z % width - half) == hop for z in range(grid.bands)]
            kept = moving if kept is None else jnp.where(jnp.array(takes)[band], moving, kept)
            kept_origin = [origin[z] if takes[z] else kept_origin[z] for z in range(grid.bands)]
        held = jnp.concatenate([held, kept])
        order = [order[z] + order[kept_origin[z]] for z in range(grid.bands)]
        width *= 2
    return held, order


def gather_couplings(grid, coupling, band, major, minor):
    rows, slots, _ = coupling.shape
    majors = grid.majors
    chunk = rows // (2 * majors)
    own = lax.dynamic_slice_in_dim(coupling, (minor * majors + major) * chunk, chunk, 0)
    gathered = []
    for slot in range(slots):
        line, order = gather_bands(grid, own[:, slot], band)
        pieces = {0: line}
        bit = majors // 2
        while bit:
            received = {
                key ^ bit: grid.send(piece, lambda z, x, m, n: (z, x, m ^ bit, n)) for key, piece in pieces.items()
            }
            pieces.update(received)
            bit //= 2
        pieces = [pieces[key] for key in range(majors)]
        if chunk % 16:
            whole = jnp.take(jnp.stack(pieces), major ^ jnp.arange(majors), axis=0)
            pieces = [whole.transpose(1, 0, 2, 3).reshape(grid.bands, rows // 2, whole.shape[3])]
        gathered.append(pieces)
    return gathered, jnp.array(order, jnp.int32)[band]


def to_columns(grid, half, band, lane, major, minor):
    rows, cols = half.shape
    bands, lanes, majors = grid.bands, grid.lanes, grid.majors
    strip = cols // majors
    part = rows // ROW_CHUNKS
    whole = jnp.zeros((bands, lanes, rows, strip), half.dtype)
    for chunk in range(ROW_CHUNKS):
        block = half[chunk * part : (chunk + 1) * part]
        first = []
        for key in range(majors):
            piece = lax.dynamic_slice(block, (0, (major ^ key) * strip), (part, strip))
            first.append(grid.send(piece, lambda z, x, m, n: (z, x, m ^ key, n)))
        first = jnp.stack(first)
        second = []
        for key in range(majors):
            piece = lax.dynamic_index_in_dim(first, (band // 2) ^ key ^ major, 0, keepdims=False)
            second.append(grid.send(piece, lambda z, x, m, n: ((z // 2 ^ key) * 2 + n, x, m, z % 2)))
        second = jnp.stack(second)
        for turn in range(lanes):
            third = grid.send(second, lambda z, x, m, n: (z, (x + turn) % lanes, m, n))
            for flip in range(2):
                fourth = third if flip == 0 else grid.send(third, lambda z, x, m, n: (z, x, m, 1 - n))
                for key in range(majors):
                    place = ((band // 2 ^ key) * 2 + (minor ^ flip), (lane - turn) % lanes, chunk * part, 0)
                    whole = lax.dynamic_update_slice(whole, fourth[key][None, None], place)
    return whole.reshape(bands * lanes * rows, strip)


def product_kernel(slots, pieces, order_ref, column_ref, count_ref, offset_ref, *refs):
    band = order_ref[pl.program_id(0)]
    coeff_ref, out_ref, mirror_ref = refs[slots * pieces :]
    chunk, tile = refs[0].shape[1:]

    def product(slot):
        first = pl.multiple_of(column_ref[band * slots + slot] * tile, tile)
        left = jnp.concatenate([refs[slot * pieces + piece][0] for piece in range(pieces)], axis=0)
        return jnp.dot(left, coeff_ref[pl.ds(first, tile), :], preferred_element_type=jnp.float32)

    def store(value, add):
        for piece in range(pieces):
            place = pl.ds(pl.multiple_of(offset_ref[piece], chunk), chunk)
            part = value[piece * chunk : (piece + 1) * chunk]
            out_ref[0, place, :] = out_ref[0, place, :] + part if add else part

    store(product(0), False)
    for slot in range(1, slots):

        @pl.when(slot < count_ref[band])
        def _():
            store(product(slot), True)

    mirror_ref[0] = out_ref[0].T


def products(couplings, columns, order, tile_columns, counts, offsets):
    slots, pieces = len(couplings), len(couplings[0])
    bands, chunk, tile = couplings[0][0].shape
    strip = columns.shape[1]
    rows = pieces * chunk
    spec = pl.BlockSpec((1, chunk, tile), lambda i, *_: (i, 0, 0))
    return pl.pallas_call(
        lambda *refs: product_kernel(slots, pieces, *refs),
        grid_spec=pltpu.PrefetchScalarGridSpec(
            num_scalar_prefetch=4,
            grid=(bands,),
            in_specs=[spec] * (slots * pieces) + [pl.BlockSpec(columns.shape, lambda i, *_: (0, 0))],
            out_specs=[
                pl.BlockSpec((1, rows, strip), lambda i, order, *_: (order[i], 0, 0)),
                pl.BlockSpec((1, strip, rows), lambda i, order, *_: (order[i], 0, 0)),
            ],
        ),
        out_shape=[
            jax.ShapeDtypeStruct((bands, rows, strip), jnp.float32),
            jax.ShapeDtypeStruct((bands, strip, rows), jnp.float32),
        ],
        compiler_params=pltpu.CompilerParams(vmem_limit_bytes=50 << 20),
        cost_estimate=pl.CostEstimate(
            flops=2 * bands * slots * rows * tile * strip,
            bytes_accessed=2 * bands * slots * rows * tile,
            transcendentals=0,
        ),
    )(order, tile_columns, counts, offsets, *[piece for slot in couplings for piece in slot], columns)


def bring_home(grid, sigma, mirrored, scale, band, lane, major, minor):
    bands, part, strip = sigma.shape
    rows, per_lane = 2 * part, grid.per_lane
    beta = major * 2 + minor
    direct = jnp.zeros((rows, grid.majors * strip), jnp.float16)
    mirror = jnp.zeros((rows, grid.majors * strip), jnp.float16)
    for key in range(bands):
        piece = lax.dynamic_index_in_dim(sigma, beta ^ key, 0, keepdims=False)
        piece = (piece * scale).astype(jnp.float16)
        piece = grid.send(piece, lambda z, x, m, n: ((m * 2 + n) ^ key, x, z // 2, z % 2))
        source = band ^ key
        direct = lax.dynamic_update_slice(direct, piece, ((source % 2) * part, (source // 2) * strip))

    def target(x, m, n):
        return (x * per_lane + m % per_lane) * 2 + n

    for key in range(bands):
        piece = lax.dynamic_index_in_dim(mirrored, target(lane, major, minor) ^ key, 0, keepdims=False)
        piece = (piece * scale).astype(jnp.float16)
        piece = grid.send(
            piece,
            lambda z, x, m, n: (z, m // per_lane, (target(x, m, n) ^ key) // 2, (target(x, m, n) ^ key) % 2),
        )
        source = beta ^ key
        place = (source // 2 % per_lane * strip, source // 2 // per_lane * rows + source % 2 * part)
        mirror = lax.dynamic_update_slice(mirror, piece, place)
    return direct, mirror


def body(coeffs, denominator, coupling, tile_cols, tile_count):
    rows = coeffs.shape[0]
    _, slots, tile = coupling.shape
    grid = Grid(lax.axis_size("alpha"), lax.axis_size("beta"))
    alpha, beta = lax.axis_index("alpha"), lax.axis_index("beta")
    band, lane = alpha // grid.lanes, alpha % grid.lanes
    major, minor = beta // 2, beta % 2
    every = jnp.arange(grid.bands, dtype=jnp.int32)
    tile_rows = (every * grid.lanes + lane) * rows // tile
    tile_columns = jnp.take(tile_cols, tile_rows, axis=0).reshape(-1)
    counts = jnp.take(tile_count, tile_rows)
    couplings, order = gather_couplings(grid, coupling, band, major, minor)
    pieces = len(couplings[0])
    offsets = (major ^ jnp.arange(pieces, dtype=jnp.int32)) * (rows // 2 // pieces)
    if pieces == 1:
        offsets = jnp.zeros((1,), jnp.int32)

    growth = slots * tile * COUPLING_MAX
    largest = jnp.maximum(largest_anywhere(grid, jnp.max(jnp.abs(coeffs))), 1e-30)
    current = coeffs
    for step_index in range(STEPS):
        scale = HALF_TOP / (growth * largest)
        largest = largest * (1 + 2 * growth / DENOMINATOR_MIN)
        columns = to_columns(grid, current.astype(jnp.bfloat16), band, lane, major, minor)
        sigma, mirrored = products(couplings, columns, order, tile_columns, counts, offsets)
        direct, mirror = bring_home(grid, sigma, mirrored, scale, band, lane, major, minor)
        total = (direct.astype(jnp.float32) + mirror.astype(jnp.float32)) / scale
        current = current - total / denominator
    return current


def solution(mesh):
    placed = (P("alpha", "beta"), P("alpha", "beta"), P("alpha", None, None), P(), P())
    return jax.shard_map(
        body, mesh=mesh, in_specs=placed, out_specs=P("alpha", "beta"), check_vma=False
    )
```

```python
import jax
import jax.numpy as jnp
from jax import lax
from jax.experimental import pallas as pl
from jax.experimental.pallas import tpu as pltpu
from jax.sharding import PartitionSpec as P

STEPS = 2
COUPLING_MAX = 0.15625
DENOMINATOR_MIN = 1.5
HALF_TOP = 60000.0
AXES = ("alpha", "beta")
ROW_CHUNKS = 4


class Grid:
    def __init__(self, alpha_devices, beta_devices):
        self.bands = beta_devices
        self.lanes = alpha_devices // beta_devices
        self.majors = beta_devices // 2
        self.per_lane = self.majors // self.lanes
        self.places = [
            (band, lane, major, minor)
            for band in range(self.bands)
            for lane in range(self.lanes)
            for major in range(self.majors)
            for minor in range(2)
        ]

    def index(self, band, lane, major, minor):
        return ((band * self.lanes + lane) * self.majors + major) * 2 + minor

    def send(self, value, where):
        pairs = [(self.index(*place), self.index(*where(*place))) for place in self.places]
        if all(source == target for source, target in pairs):
            return value
        return lax.ppermute(value, AXES, pairs)


def after(value, *earlier):
    return lax.optimization_barrier((value, *earlier))[0]


def largest_anywhere(grid, value, gates):
    devices = len(grid.places)
    largest = jnp.full((8, 128), value)
    bit = 1
    while bit < devices:
        pairs = [(device, device ^ bit) for device in range(devices)]
        largest = after(largest, gates[min(bit.bit_length(), len(gates)) - 1])
        largest = jnp.maximum(largest, lax.ppermute(largest, AXES, pairs))
        bit *= 2
    return largest[0, 0]


def gather_bands(grid, own, band, gate):
    held = own[None] if gate is None else after(own[None], gate)
    swaps = []
    order = [[z] for z in range(grid.bands)]
    width = 2
    while width <= grid.bands:
        half = width // 2
        moving = held
        origin = list(range(grid.bands))
        kept, kept_origin = None, [None] * grid.bands
        for hop in range(half):
            partner = list(range(grid.bands))
            for base in range(0, grid.bands, width):
                low, high = base + half - 1, base + half
                if hop == 0:
                    pairs = [(low, high)]
                else:
                    pairs = [(low - hop + 1, low - hop), (high + hop - 1, high + hop)]
                for one, other in pairs:
                    partner[one], partner[other] = other, one
            moving = grid.send(moving, lambda z, x, m, n: (partner[z], x, m, n))
            if hop == 0:
                swaps.append(moving)
            origin = [origin[partner[z]] for z in range(grid.bands)]
            takes = [(half - 1 - z % width if z % width < half else z % width - half) == hop for z in range(grid.bands)]
            kept = moving if kept is None else jnp.where(jnp.array(takes)[band], moving, kept)
            kept_origin = [origin[z] if takes[z] else kept_origin[z] for z in range(grid.bands)]
        held = jnp.concatenate([held, kept])
        order = [order[z] + order[kept_origin[z]] for z in range(grid.bands)]
        width *= 2
    return held, order, swaps


def gather_couplings(grid, coupling, band, major, minor):
    rows, slots, _ = coupling.shape
    majors = grid.majors
    chunk = rows // (2 * majors)
    own = lax.dynamic_slice_in_dim(coupling, (minor * majors + major) * chunk, chunk, 0)
    gathered, swaps, gate = [], [], None
    for slot in range(slots):
        line, order, swapped = gather_bands(grid, own[:, slot], band, gate)
        gate = swapped[0]
        swaps.append(swapped[-1])
        pieces = {0: line}
        bit = majors // 2
        while bit:
            received = {
                key ^ bit: grid.send(piece, lambda z, x, m, n: (z, x, m ^ bit, n)) for key, piece in pieces.items()
            }
            pieces.update(received)
            bit //= 2
        pieces = [pieces[key] for key in range(majors)]
        if chunk % 16:
            whole = jnp.take(jnp.stack(pieces), major ^ jnp.arange(majors), axis=0)
            pieces = [whole.transpose(1, 0, 2, 3).reshape(grid.bands, rows // 2, whole.shape[3])]
        gathered.append(pieces)
    return gathered, jnp.array(order, jnp.int32)[band], swaps


def to_columns(grid, half, band, lane, major, minor, gate):
    rows, cols = half.shape
    lanes, majors = grid.lanes, grid.majors
    strip = cols // majors
    part = rows // ROW_CHUNKS
    parts, places = [], []
    for chunk in range(ROW_CHUNKS):
        block = half[chunk * part : (chunk + 1) * part]
        first = []
        for key in range(majors):
            piece = lax.dynamic_slice(block, (0, (major ^ key) * strip), (part, strip))
            first.append(grid.send(piece, lambda z, x, m, n: (z, x, m ^ key, n)))
        first = jnp.stack(first)
        if gate is not None:
            first = after(first, gate)
        second = []
        for key in range(majors):
            piece = lax.dynamic_index_in_dim(first, (band // 2) ^ key ^ major, 0, keepdims=False)
            second.append(grid.send(piece, lambda z, x, m, n: ((z // 2 ^ key) * 2 + n, x, m, z % 2)))
        second = jnp.stack(second)
        for turn in range(lanes):
            third = grid.send(second, lambda z, x, m, n: (z, (x + turn) % lanes, m, n))
            for flip in range(2):
                parts.append(third if flip == 0 else grid.send(third, lambda z, x, m, n: (z, x, m, 1 - n)))
                for key in range(majors):
                    alpha = ((band // 2 ^ key) * 2 + (minor ^ flip)) * lanes + (lane - turn) % lanes
                    places.append(alpha * rows + chunk * part)
    return parts, jnp.stack(places)


def product_kernel(slots, pieces, order_ref, entry_ref, column_ref, count_ref, offset_ref, place_ref, scale_ref, *refs):
    couplings, parts = refs[: slots * pieces], refs[slots * pieces : -4]
    out_ref, mirror_ref, coeff_ref, sems = refs[-4:]
    band = order_ref[pl.program_id(0)]
    chunk, tile = couplings[0].shape[1:]
    majors, part, _ = parts[0].shape

    @pl.when(pl.program_id(0) == 0)
    def _():
        copies = []
        for i in range(len(parts) * majors):
            place = pl.ds(pl.multiple_of(place_ref[i], part), part)
            source = parts[i // majors].at[i % majors]
            copies.append(pltpu.make_async_copy(source, coeff_ref.at[place], sems.at[i]))
        for copy in copies:
            copy.start()
        for copy in copies:
            copy.wait()

    def product(slot):
        first = pl.multiple_of(column_ref[band * slots + slot] * tile, tile)
        left = jnp.concatenate([couplings[slot * pieces + piece][0] for piece in range(pieces)], axis=0)
        return jnp.dot(left, coeff_ref[pl.ds(first, tile), :], preferred_element_type=jnp.float32) * scale_ref[0]

    def store(value, add):
        for piece in range(pieces):
            place = pl.ds(pl.multiple_of(offset_ref[piece], chunk), chunk)
            part = value[piece * chunk : (piece + 1) * chunk]
            out_ref[0, place, :] = out_ref[0, place, :] + part if add else part

    store(product(0), False)
    for slot in range(1, slots):

        @pl.when(slot < count_ref[band])
        def _():
            store(product(slot), True)

    mirror_ref[0] = out_ref[0].T


def products(couplings, parts, order, entries, tile_columns, counts, offsets, places, scale):
    slots, pieces = len(couplings), len(couplings[0])
    _, chunk, tile = couplings[0][0].shape
    majors, part, strip = parts[0].shape
    rows, calls = pieces * chunk, order.shape[0]
    spec = pl.BlockSpec((1, chunk, tile), lambda i, order, entry, *_: (entry[i], 0, 0))
    return pl.pallas_call(
        lambda *refs: product_kernel(slots, pieces, *refs),
        grid_spec=pltpu.PrefetchScalarGridSpec(
            num_scalar_prefetch=7,
            grid=(calls,),
            in_specs=[spec] * (slots * pieces) + [pl.BlockSpec(memory_space=pl.ANY)] * len(parts),
            out_specs=[
                pl.BlockSpec((1, rows, strip), lambda i, *_: (i, 0, 0)),
                pl.BlockSpec((1, strip, rows), lambda i, *_: (i, 0, 0)),
            ],
            scratch_shapes=[
                pltpu.VMEM((len(parts) * majors * part, strip), jnp.bfloat16),
                pltpu.SemaphoreType.DMA((len(parts) * majors,)),
            ],
        ),
        out_shape=[
            jax.ShapeDtypeStruct((calls, rows, strip), jnp.float32),
            jax.ShapeDtypeStruct((calls, strip, rows), jnp.float32),
        ],
        compiler_params=pltpu.CompilerParams(vmem_limit_bytes=40 << 20),
        cost_estimate=pl.CostEstimate(
            flops=2 * calls * slots * rows * tile * strip,
            bytes_accessed=2 * (calls * slots * rows * tile + len(parts) * majors * part * strip),
            transcendentals=0,
        ),
    )(
        order,
        entries,
        tile_columns,
        counts,
        offsets,
        places,
        scale[None],
        *[piece for slot in couplings for piece in slot],
        *parts,
    )


def bring_home(grid, halves, band, lane, major, minor):
    bands, per_lane = grid.bands, grid.per_lane
    run, part, strip = halves[0][0].shape
    rows = 2 * part
    beta = major * 2 + minor
    direct = jnp.zeros((rows, grid.majors * strip), jnp.float16)
    mirror = jnp.zeros((rows, grid.majors * strip), jnp.float16)
    for key in range(bands):
        piece = halves[key // run][0][key % run].astype(jnp.float16)
        piece = grid.send(piece, lambda z, x, m, n: ((m * 2 + n) ^ key, x, z // 2, z % 2))
        source = band ^ key
        direct = lax.dynamic_update_slice(direct, piece, (source % 2 * part, source // 2 * strip))

    def target(x, m, n):
        return (x * per_lane + m % per_lane) * 2 + n

    for key in range(bands):
        entry = target(lane, major, minor) ^ key ^ beta
        piece = [lax.dynamic_index_in_dim(half[1], entry % run, 0, keepdims=False) for half in halves]
        piece = jnp.where(entry // run == 0, *piece).astype(jnp.float16)
        piece = grid.send(
            piece,
            lambda z, x, m, n: (z, m // per_lane, (target(x, m, n) ^ key) // 2, (target(x, m, n) ^ key) % 2),
        )
        source = beta ^ key
        place = (source // 2 % per_lane * strip, (source // 2 // per_lane * 2 + source % 2) * part)
        mirror = lax.dynamic_update_slice(mirror, piece, place)
    return direct, mirror


def body(coeffs, denominator, coupling, tile_cols, tile_count):
    rows = coeffs.shape[0]
    _, slots, tile = coupling.shape
    grid = Grid(lax.axis_size("alpha"), lax.axis_size("beta"))
    alpha, beta = lax.axis_index("alpha"), lax.axis_index("beta")
    band, lane = alpha // grid.lanes, alpha % grid.lanes
    major, minor = beta // 2, beta % 2
    every = jnp.arange(grid.bands, dtype=jnp.int32)
    tile_rows = (every * grid.lanes + lane) * rows // tile
    tile_columns = jnp.take(tile_cols, tile_rows, axis=0).reshape(-1)
    counts = jnp.take(tile_count, tile_rows)
    half = coeffs.astype(jnp.bfloat16)
    couplings, order, swaps = gather_couplings(grid, coupling, band, major, minor)
    pieces = len(couplings[0])
    offsets = (major ^ jnp.arange(pieces, dtype=jnp.int32)) * (rows // 2 // pieces)
    if pieces == 1:
        offsets = jnp.zeros((1,), jnp.int32)
    wanted = beta ^ every
    entries = jnp.argmax(order[None, :] == wanted[:, None], axis=1).astype(jnp.int32)

    growth = slots * tile * COUPLING_MAX
    largest = jnp.maximum(largest_anywhere(grid, jnp.max(jnp.abs(coeffs)), swaps), 1e-30)
    current = coeffs
    gate = swaps[-1]
    for step_index in range(STEPS):
        scale = HALF_TOP / (growth * largest)
        largest = largest * (1 + 2 * growth / DENOMINATOR_MIN)
        parts, places = to_columns(grid, half, band, lane, major, minor, gate)
        gate = None
        runs = [slice(0, grid.bands // 2), slice(grid.bands // 2, grid.bands)]
        halves = [
            products(couplings, parts, wanted[run], entries[run], tile_columns, counts, offsets, places, scale)
            for run in runs
        ]
        direct, mirror = bring_home(grid, halves, band, lane, major, minor)
        total = (direct.astype(jnp.float32) + mirror.astype(jnp.float32)) / scale
        current = current - total / denominator
        half = current.astype(jnp.bfloat16)
    return current


def solution(mesh):
    placed = (P("alpha", "beta"), P("alpha", "beta"), P("alpha", None, None), P(), P())
    return jax.shard_map(
        body, mesh=mesh, in_specs=placed, out_specs=P("alpha", "beta"), check_vma=False
    )
```

```python
import jax
import jax.numpy as jnp
from jax import lax
from jax.experimental import pallas as pl
from jax.experimental.pallas import tpu as pltpu
from jax.sharding import PartitionSpec as P

STEPS = 2
COUPLING_MAX = 0.15625
DENOMINATOR_MIN = 1.5
HALF_TOP = 60000.0
AXES = ("alpha", "beta")
ROW_CHUNKS = 3


class Grid:
    def __init__(self, alpha_devices, beta_devices):
        self.bands = beta_devices
        self.lanes = alpha_devices // beta_devices
        self.majors = beta_devices // 2
        self.per_lane = self.majors // self.lanes
        self.places = [
            (band, lane, major, minor)
            for band in range(self.bands)
            for lane in range(self.lanes)
            for major in range(self.majors)
            for minor in range(2)
        ]

    def index(self, band, lane, major, minor):
        return ((band * self.lanes + lane) * self.majors + major) * 2 + minor

    def send(self, value, where, idle=None):
        stays = [where(*place) == place for place in self.places]
        if all(stays):
            return value
        pairs = []
        for place, stay in zip(self.places, stays):
            target = idle(*place) if stay else where(*place)
            pairs.append((self.index(*place), self.index(*target)))
        received = lax.ppermute(value, AXES, pairs)
        if any(stays):
            device = lax.axis_index("alpha") * self.bands + lax.axis_index("beta")
            received = jnp.where(jnp.array(stays)[device], value, received)
        return received


def after(value, *earlier):
    return lax.optimization_barrier((value, *earlier))[0]


def other_minor(z, x, m, n):
    return (z, x, m, 1 - n)


def gather_bands(grid, own, band, busy=None):
    held = own[None]
    swaps = []
    order = [[z] for z in range(grid.bands)]
    width = 2
    while width <= grid.bands:
        half = width // 2
        moving = held
        origin = list(range(grid.bands))
        kept, kept_origin = None, [None] * grid.bands
        for hop in range(half):
            partner = list(range(grid.bands))
            for base in range(0, grid.bands, width):
                low, high = base + half - 1, base + half
                if hop == 0:
                    pairs = [(low, high)]
                else:
                    pairs = [(low - hop + 1, low - hop), (high + hop - 1, high + hop)]
                for one, other in pairs:
                    partner[one], partner[other] = other, one
            pairs = [
                (grid.index(z, x, m, n), grid.index(partner[z], x, m, 1 - n if partner[z] == z else n))
                for z, x, m, n in grid.places
            ]
            moving = lax.ppermute(moving, AXES, pairs)
            if hop == 0:
                swaps.append(moving)
            origin = [origin[partner[z]] for z in range(grid.bands)]
            takes = [(half - 1 - z % width if z % width < half else z % width - half) == hop for z in range(grid.bands)]
            kept = moving if kept is None else jnp.where(jnp.array(takes)[band], moving, kept)
            kept_origin = [origin[z] if takes[z] else kept_origin[z] for z in range(grid.bands)]
        if busy is None:
            held = jnp.concatenate([held, kept])
        else:
            mine = jnp.any(busy & (jnp.arange(grid.bands) // half == band // half))
            held = jnp.where(mine, held, kept)
        order = [order[z] + order[kept_origin[z]] for z in range(grid.bands)]
        width *= 2
    return held, order, swaps


def spread_majors(grid, line):
    pieces = {0: line}
    bit = grid.majors // 2
    while bit:
        received = {key ^ bit: grid.send(piece, lambda z, x, m, n: (z, x, m ^ bit, n)) for key, piece in pieces.items()}
        pieces.update(received)
        bit //= 2
    return [pieces[key] for key in range(grid.majors)]


def spread_inputs(grid, coupling, half, extreme, busy, band, lane, major, minor):
    rows, slots, tile = coupling.shape
    chunk = rows // (2 * grid.majors)
    first = (minor * grid.majors + major) * chunk
    dense = slots if busy is None else slots // 2
    groups = [(slot, 1) for slot in range(dense)]
    if busy is not None:
        groups.append((dense, slots - dense))
    extreme = jnp.full((16, tile), extreme)
    for where in (lambda z, x, m, n: (z, (x + 1) % grid.lanes, m, n), other_minor):
        extreme = jnp.maximum(extreme, grid.send(extreme, where))
    lines, swaps, gate = [], [], None
    for number, (slot, count) in enumerate(groups):
        source = coupling if gate is None else after(coupling, gate)
        own = lax.dynamic_slice_in_dim(source, first, chunk, 0)[:, slot : slot + count].transpose(1, 0, 2)
        if number == 1:
            own = jnp.concatenate([own, extreme[None]], axis=1)
        line, line_order, swapped = gather_bands(grid, own, band, None if slot < dense else busy)
        gate = swapped[0]
        swaps.append(swapped[-1])
        lines.append(line)
        if slot < dense:
            order = line_order
    gathered = [spread_majors(grid, line) for line in lines]
    rode = [piece[:, 0, chunk, 0] for piece in gathered[1]]
    largest = jnp.max(jnp.stack(rode)).astype(jnp.float32)
    gates = [swaps[1], gathered[0][-1], gathered[1][-1]]
    parts, places = to_columns(grid, half, band, lane, major, minor, gates, True)
    result = []
    for (slot, count), pieces in zip(groups, gathered):
        if slot >= dense:
            pieces = [jnp.broadcast_to(piece, (grid.bands, *piece.shape[1:])) for piece in pieces]
        if chunk % 16:
            whole = jnp.take(jnp.stack(pieces), major ^ jnp.arange(grid.majors), axis=0)[:, :, :, :chunk]
            pieces = [whole.transpose(1, 2, 0, 3, 4).reshape(grid.bands, count, rows // 2, tile)]
        for i in range(count):
            result.append([piece[:, i] for piece in pieces])
    return result, jnp.array(order, jnp.int32)[band], largest, parts, places


def to_columns(grid, half, band, lane, major, minor, gates, by_lane):
    def idle(z, x, m, n):
        return (z, (x + 1) % lanes, m, n) if by_lane else (z, x, m ^ 1, n)

    rows, cols = half.shape
    lanes, majors = grid.lanes, grid.majors
    strip = cols // majors
    part = rows // ROW_CHUNKS
    parts, places = [], []
    for chunk in range(ROW_CHUNKS):
        block = half[chunk * part : (chunk + 1) * part]
        first = []
        for key in range(majors):
            piece = lax.dynamic_slice(block, (0, (major ^ key) * strip), (part, strip))
            first.append(grid.send(piece, lambda z, x, m, n: (z, x, m ^ key, n)))
        first = jnp.stack(first)
        if gates:
            first = after(first, gates[min(chunk, len(gates) - 1)])
        second = []
        for key in range(majors):
            piece = lax.dynamic_index_in_dim(first, (band // 2) ^ key ^ major, 0, keepdims=False)
            second.append(grid.send(piece, lambda z, x, m, n: ((z // 2 ^ key) * 2 + n, x, m, z % 2), idle))
        second = jnp.stack(second)
        for turn in range(lanes):
            third = grid.send(second, lambda z, x, m, n: (z, (x + turn) % lanes, m, n))
            for flip in range(2):
                parts.append(third if flip == 0 else grid.send(third, lambda z, x, m, n: (z, x, m, 1 - n)))
                for key in range(majors):
                    alpha = ((band // 2 ^ key) * 2 + (minor ^ flip)) * lanes + (lane - turn) % lanes
                    places.append(alpha * rows + chunk * part)
    return parts, jnp.stack(places)


def product_kernel(slots, pieces, order_ref, entry_ref, column_ref, count_ref, offset_ref, place_ref, scale_ref, *refs):
    couplings, parts = refs[: slots * pieces], refs[slots * pieces : -4]
    out_ref, mirror_ref, coeff_ref, sems = refs[-4:]
    band = order_ref[pl.program_id(0)]
    chunk = out_ref.shape[1] // pieces
    tile = couplings[0].shape[2]
    majors, part, _ = parts[0].shape

    @pl.when(pl.program_id(0) == 0)
    def _():
        copies = []
        for i in range(len(parts) * majors):
            place = pl.ds(pl.multiple_of(place_ref[i], part), part)
            source = parts[i // majors].at[i % majors]
            copies.append(pltpu.make_async_copy(source, coeff_ref.at[place], sems.at[i]))
        for copy in copies:
            copy.start()
        for copy in copies:
            copy.wait()

    def product(slot):
        first = pl.multiple_of(column_ref[band * slots + slot] * tile, tile)
        left = jnp.concatenate([couplings[slot * pieces + piece][0, :chunk] for piece in range(pieces)], axis=0)
        return jnp.dot(left, coeff_ref[pl.ds(first, tile), :], preferred_element_type=jnp.float32) * scale_ref[0]

    def store(value, add):
        for piece in range(pieces):
            place = pl.ds(pl.multiple_of(offset_ref[piece], chunk), chunk)
            part = value[piece * chunk : (piece + 1) * chunk]
            out_ref[0, place, :] = out_ref[0, place, :] + part if add else part

    store(product(0), False)
    for slot in range(1, slots):

        @pl.when(slot < count_ref[band])
        def _():
            store(product(slot), True)

    mirror_ref[0] = out_ref[0].T


def products(couplings, parts, order, entries, tile_columns, counts, offsets, places, scale):
    slots, pieces = len(couplings), len(couplings[0])
    tile = couplings[0][0].shape[2]
    majors, part, strip = parts[0].shape
    chunk = part * ROW_CHUNKS // 2 // pieces
    rows, calls = pieces * chunk, order.shape[0]
    spec = pl.BlockSpec((1, chunk, tile), lambda i, order, entry, *_: (entry[i], 0, 0))
    return pl.pallas_call(
        lambda *refs: product_kernel(slots, pieces, *refs),
        grid_spec=pltpu.PrefetchScalarGridSpec(
            num_scalar_prefetch=7,
            grid=(calls,),
            in_specs=[spec] * (slots * pieces) + [pl.BlockSpec(memory_space=pltpu.HBM)] * len(parts),
            out_specs=[
                pl.BlockSpec((1, rows, strip), lambda i, *_: (i, 0, 0)),
                pl.BlockSpec((1, strip, rows), lambda i, *_: (i, 0, 0)),
            ],
            scratch_shapes=[
                pltpu.VMEM((len(parts) * majors * part, strip), jnp.bfloat16),
                pltpu.SemaphoreType.DMA((len(parts) * majors,)),
            ],
        ),
        out_shape=[
            jax.ShapeDtypeStruct((calls, rows, strip), jnp.float32),
            jax.ShapeDtypeStruct((calls, strip, rows), jnp.float32),
        ],
        compiler_params=pltpu.CompilerParams(vmem_limit_bytes=40 << 20),
        cost_estimate=pl.CostEstimate(
            flops=2 * calls * slots * rows * tile * strip,
            bytes_accessed=2 * (calls * slots * rows * tile + len(parts) * majors * part * strip),
            transcendentals=0,
        ),
    )(
        order,
        entries,
        tile_columns,
        counts,
        offsets,
        places,
        scale[None],
        *[piece for slot in couplings for piece in slot],
        *parts,
    )


def bring_home(grid, halves, band, lane, major, minor):
    bands, per_lane = grid.bands, grid.per_lane
    run, part, strip = halves[0][0].shape
    rows = 2 * part
    beta = major * 2 + minor
    mirror = jnp.zeros((rows, grid.majors * strip), jnp.float16)
    received = []
    for key in range(bands):
        piece = halves[key // run][0][key % run].astype(jnp.float16)
        received.append(
            grid.send(
                piece,
                lambda z, x, m, n: ((m * 2 + n) ^ key, x, z // 2, z % 2),
                lambda z, x, m, n: (z, (x + 1) % grid.lanes, m, n),
            )
        )
    direct = jnp.zeros((rows, grid.majors * strip), jnp.float16)
    for key in range(grid.majors):
        one, other = received[2 * key : 2 * key + 2]
        even = band % 2 == 0
        pair = jnp.concatenate([jnp.where(even, one, other), jnp.where(even, other, one)])
        direct = lax.dynamic_update_slice_in_dim(direct, pair, (band // 2 ^ key) * strip, 1)

    def target(x, m, n):
        return (x * per_lane + m % per_lane) * 2 + n

    for key in range(bands):
        entry = target(lane, major, minor) ^ key ^ beta
        piece = [lax.dynamic_index_in_dim(half[1], entry % run, 0, keepdims=False) for half in halves]
        piece = jnp.where(entry // run == 0, *piece).astype(jnp.float16)
        piece = grid.send(
            piece,
            lambda z, x, m, n: (z, m // per_lane, (target(x, m, n) ^ key) // 2, (target(x, m, n) ^ key) % 2),
            other_minor,
        )
        source = beta ^ key
        place = (source // 2 % per_lane * strip, (source // 2 // per_lane * 2 + source % 2) * part)
        mirror = lax.dynamic_update_slice(mirror, piece, place)
    return direct, mirror


def body(coeffs, denominator, coupling, tile_cols, tile_count):
    rows = coeffs.shape[0]
    _, slots, tile = coupling.shape
    grid = Grid(lax.axis_size("alpha"), lax.axis_size("beta"))
    alpha, beta = lax.axis_index("alpha"), lax.axis_index("beta")
    band, lane = alpha // grid.lanes, alpha % grid.lanes
    major, minor = beta // 2, beta % 2
    every = jnp.arange(grid.bands, dtype=jnp.int32)
    tile_rows = (every * grid.lanes + lane) * rows // tile
    tile_columns = jnp.take(tile_cols, tile_rows, axis=0).reshape(-1)
    counts = jnp.take(tile_count, tile_rows)
    half = coeffs.astype(jnp.bfloat16)
    extreme = (jnp.maximum(jnp.max(jnp.abs(coeffs)), 1e-30) * 1.01).astype(jnp.bfloat16)
    all_rows = (jnp.arange(grid.bands * grid.lanes) * rows // tile).reshape(grid.bands, grid.lanes)
    many = jnp.take(tile_count, all_rows) > slots // 2
    busy = jnp.take(many, lane, axis=1)

    def one_busy(*values):
        return spread_inputs(grid, *values, busy, band, lane, major, minor)

    def any_busy(*values):
        return spread_inputs(grid, *values, None, band, lane, major, minor)

    couplings, order, largest, parts, places = lax.cond(
        jnp.max(jnp.sum(many, axis=0)) <= 1, one_busy, any_busy, coupling, half, extreme
    )
    pieces = len(couplings[0])
    offsets = (major ^ jnp.arange(pieces, dtype=jnp.int32)) * (rows // 2 // pieces)
    if pieces == 1:
        offsets = jnp.zeros((1,), jnp.int32)
    wanted = beta ^ every
    entries = jnp.argmax(order[None, :] == wanted[:, None], axis=1).astype(jnp.int32)

    growth = slots * tile * COUPLING_MAX
    current = coeffs
    for step_index in range(STEPS):
        scale = HALF_TOP / (growth * largest)
        largest = largest * (1 + 2 * growth / DENOMINATOR_MIN)
        if step_index:
            half = current.astype(jnp.bfloat16)
            parts, places = to_columns(grid, half, band, lane, major, minor, [], False)
        runs = [slice(0, grid.bands // 2), slice(grid.bands // 2, grid.bands)]
        halves = [
            products(couplings, parts, wanted[run], entries[run], tile_columns, counts, offsets, places, scale)
            for run in runs
        ]
        direct, mirror = bring_home(grid, halves, band, lane, major, minor)
        total = (direct.astype(jnp.float32) + mirror.astype(jnp.float32)) / scale
        current = current - total / denominator
    return current


def solution(mesh):
    placed = (P("alpha", "beta"), P("alpha", "beta"), P("alpha", None, None), P(), P())
    return jax.shard_map(
        body, mesh=mesh, in_specs=placed, out_specs=P("alpha", "beta"), check_vma=False
    )
```

```python
import jax
import jax.numpy as jnp
from jax import lax
from jax.experimental import pallas as pl
from jax.experimental.pallas import tpu as pltpu
from jax.sharding import PartitionSpec as P

STEPS = 2
COUPLING_MAX = 0.15625
DENOMINATOR_MIN = 1.5
HALF_TOP = 60000.0
AXES = ("alpha", "beta")
ROW_CHUNKS = 4


class Grid:
    def __init__(self, alpha_devices, beta_devices):
        self.bands = beta_devices
        self.lanes = alpha_devices // beta_devices
        self.majors = beta_devices // 2
        self.places = [
            (band, lane, major, minor)
            for band in range(self.bands)
            for lane in range(self.lanes)
            for major in range(self.majors)
            for minor in range(2)
        ]

    def index(self, band, lane, major, minor):
        return ((band * self.lanes + lane) * self.majors + major) * 2 + minor

    def send(self, value, where, idle=None):
        stays = [where(*place) == place for place in self.places]
        if all(stays):
            return value
        pairs = []
        for place, stay in zip(self.places, stays):
            target = idle(*place) if stay else where(*place)
            pairs.append((self.index(*place), self.index(*target)))
        received = lax.ppermute(value, AXES, pairs)
        if any(stays):
            device = lax.axis_index("alpha") * self.bands + lax.axis_index("beta")
            received = jnp.where(jnp.array(stays)[device], value, received)
        return received


def after(value, *earlier):
    earlier = [array for array in earlier if array is not None]
    return lax.optimization_barrier((value, *earlier))[0] if earlier else value


def bits(count):
    return [1 << i for i in reversed(range(count.bit_length() - 1))]


def ordered(entries, me):
    if len(entries) == 1:
        return entries
    half = len(entries) // 2
    near, far = ordered(entries[:half], me), ordered(entries[half:], me)
    low = (me & half) == 0
    pairs = list(zip(near, far))
    return [jnp.where(low, a, b) for a, b in pairs] + [jnp.where(low, b, a) for a, b in pairs]


def line_order(bands):
    order, half = [[z] for z in range(bands)], 1
    while half < bands:
        middle = [z // (2 * half) * 2 * half + half - (z // half % 2) for z in range(bands)]
        order, half = [order[z] + order[middle[z]] for z in range(bands)], 2 * half
    return order


def gather_bands(grid, own, band, busy=None):
    held = own[None]
    brought = []
    width = 2
    while width <= grid.bands:
        half = width // 2
        moving, kept = held, None
        for hop in range(half):
            partner = list(range(grid.bands))
            for base in range(0, grid.bands, width):
                low, high = base + half - 1, base + half
                if hop == 0:
                    pairs = [(low, high)]
                else:
                    pairs = [(low - hop + 1, low - hop), (high + hop - 1, high + hop)]
                for one, other in pairs:
                    partner[one], partner[other] = other, one
            pairs = [
                (grid.index(z, x, m, n), grid.index(partner[z], x, m, 1 - n if partner[z] == z else n))
                for z, x, m, n in grid.places
            ]
            moving = lax.ppermute(moving, AXES, pairs)
            if hop == 0:
                brought.append(moving)
            takes = [(half - 1 - z % width if z % width < half else z % width - half) == hop for z in range(grid.bands)]
            kept = moving if kept is None else jnp.where(jnp.array(takes)[band], moving, kept)
        if busy is None:
            held = jnp.concatenate([held, kept])
        else:
            mine = jnp.any(busy & (jnp.arange(grid.bands) // half == band // half))
            held = jnp.where(mine, held, kept)
        width *= 2
    return held, brought


def spread_majors(grid, line):
    pieces = {0: line}
    for bit in bits(grid.majors):
        received = {key ^ bit: grid.send(piece, lambda z, x, m, n: (z, x, m ^ bit, n)) for key, piece in pieces.items()}
        pieces.update(received)
    return [pieces[key] for key in range(grid.majors)]


def spread_inputs(grid, coupling, coeffs, busy, band, lane, major, minor):
    rows, slots, tile = coupling.shape
    chunk = rows // (2 * grid.majors)
    first = (minor * grid.majors + major) * chunk
    dense = slots if busy is None else slots // 2
    groups = [(slot, 1) for slot in range(dense)]
    if busy is not None:
        groups.append((dense, slots - dense))
    rider = 1
    lines, gates = [], [None]
    half, extreme = None, None
    for number, (slot, count) in enumerate(groups):
        source = after(coupling, gates[-1])
        own = [lax.dynamic_slice(source, (first, slot + i, 0), (chunk, 1, tile)) for i in range(count)]
        own = jnp.concatenate([one.reshape(1, chunk, tile) for one in own])
        if number == 0:
            values = after(coeffs, own)
            half = values.astype(jnp.bfloat16)
            extreme = (jnp.maximum(jnp.max(jnp.abs(values)), 1e-30) * 1.01).astype(jnp.bfloat16)
            extreme = jnp.full((16, tile), extreme)
        if number == rider:
            for where in (lambda z, x, m, n: (z, x, m, 1 - n), lambda z, x, m, n: (z, (x + 1) % grid.lanes, m, n)):
                extreme = jnp.maximum(extreme, grid.send(extreme, where))
            own = jnp.concatenate([own, jnp.broadcast_to(extreme, (count, *extreme.shape))], axis=1)
        line, brought = gather_bands(grid, own, band, None if slot < dense else busy)
        gates.append(brought[0])
        lines.append((line, brought))
    gathered = [spread_majors(grid, line) for line, _ in lines]
    rode = [piece[:, 0, chunk, 0] for piece in gathered[rider]]
    largest = jnp.max(jnp.stack(rode)).astype(jnp.float32)
    z_gates = [lines[0][0], lines[1][1][-1], gathered[0][-1], gathered[1][-1]]
    parts = to_columns(grid, half, band, lane, major, minor, z_gates, [ROW_CHUNKS], True)
    result = []
    for (slot, count), pieces in zip(groups, gathered):
        if slot >= dense:
            pieces = [jnp.broadcast_to(piece, (grid.bands, *piece.shape[1:])) for piece in pieces]
        if chunk % 16:
            whole = jnp.take(jnp.stack(pieces), major ^ jnp.arange(grid.majors), axis=0)[:, :, :, :chunk]
            pieces = [whole.transpose(1, 2, 0, 3, 4).reshape(grid.bands, count, rows // 2, tile)]
        result.append(pieces)
    if busy is None:
        late, result = result[dense // 2 :], result[: dense // 2]
        kept = rows // 2 // len(late[0])
        joined = [jnp.concatenate([one[:, :, :kept] for one in ones], axis=1) for ones in zip(*late)]
        result.append(joined)
    return result, largest, parts


def to_columns(grid, half, band, lane, major, minor, gates, batches, by_lane):
    rows = half.shape[0]
    lanes, majors = grid.lanes, grid.majors
    part, share = rows // ROW_CHUNKS, rows // majors

    def idle(z, x, m, n):
        return (z, (x + 1) % lanes, m, n) if by_lane else (z, x, m ^ 1, n)

    firsts, done = [], 0
    for batch in batches:
        block = half[done * part : (done + batch) * part]
        first = []
        for key in range(majors):
            piece = [
                lax.dynamic_slice_in_dim(block, (x * majors + (major ^ key)) * share, share, 1) for x in range(lanes)
            ]
            first.append(grid.send(jnp.concatenate(piece, 1), lambda z, x, m, n: (z, x, m ^ key, n)))
        firsts += [[one[i * part : (i + 1) * part] for one in first] for i in range(batch)]
        done += batch
    parts, earlier = [], [None] * majors
    for chunk, first in enumerate(firsts):
        first = jnp.stack(first)
        second = []
        for key in range(majors):
            piece = lax.dynamic_index_in_dim(first, (band // 2) ^ key ^ major, 0, keepdims=False)
            piece = after(piece, earlier[key], gates[min(chunk, len(gates) - 1)] if gates else None)
            piece = grid.send(piece, lambda z, x, m, n: ((z // 2 ^ key) * 2 + n, x, m, z % 2), idle)
            earlier[key] = piece
            second.append(piece)
        second = jnp.stack(second)
        for turn in range(lanes):
            third = grid.send(second, lambda z, x, m, n: (z, (x + turn) % lanes, m, n))
            parts += [third, grid.send(third, lambda z, x, m, n: (z, x, m, 1 - n))]
    return parts


def product_kernel(groups, pieces, lanes, base, id_ref, entry_ref, column_ref, count_ref, scale_ref, *refs):
    couplings, parts = refs[: len(groups) * pieces], refs[len(groups) * pieces : -4]
    out_ref, mirror_ref, coeff_ref, sems = refs[-4:]
    band, lane, major, minor = (id_ref[i] for i in range(4))
    chunk = out_ref.shape[1] // pieces
    tile = couplings[0].shape[3]
    majors, part, _ = parts[0].shape
    bands, rows = 2 * majors, part * ROW_CHUNKS
    wanted = (major * 2 + minor) ^ (base + pl.program_id(0))
    tile_row = (wanted * lanes + lane) * rows // tile

    @pl.when(pl.program_id(0) == 0)
    def _():
        copies = []
        for i, ref in enumerate(parts):
            turn, flip = i // 2 % lanes, i % 2
            for key in range(majors):
                alpha = (((band // 2) ^ key) * 2 + (minor ^ flip)) * lanes + lax.rem(lane + lanes - turn, lanes)
                first = pl.multiple_of(alpha * rows + i // (2 * lanes) * part, part)
                target = coeff_ref.at[pl.ds(first, part)]
                copies.append(pltpu.make_async_copy(ref.at[key], target, sems.at[i * majors + key]))
        for copy in copies:
            copy.start()
        for copy in copies:
            copy.wait()

    def product(number, i, slot):
        first = pl.multiple_of(column_ref[tile_row * sum(groups) + slot] * tile, tile)
        left = [couplings[number * pieces + piece][0, i, :chunk] for piece in range(pieces)]
        left = jnp.concatenate(left, axis=0)
        return jnp.dot(left, coeff_ref[pl.ds(first, tile), :], preferred_element_type=jnp.float32) * scale_ref[0]

    def store(value, add):
        for piece in range(pieces):
            first = (major ^ piece) * chunk if pieces > 1 else 0
            place = pl.ds(pl.multiple_of(first, chunk), chunk)
            rows_of = value[piece * chunk : (piece + 1) * chunk]
            out_ref[0, place, :] = out_ref[0, place, :] + rows_of if add else rows_of

    slot = 0
    for number, count in enumerate(groups):
        for i in range(count):
            if slot == 0:
                store(product(number, i, slot), False)
            else:
                pl.when(slot < count_ref[tile_row])(lambda: store(product(number, i, slot), True))
            slot += 1

    mirror_ref[0] = out_ref[0].T


def products(grid, couplings, parts, ids, entries, tile_cols, tile_count, scale, base):
    bands, lanes = grid.bands, grid.lanes
    groups, pieces = [group[0].shape[1] for group in couplings], len(couplings[0])
    tile = couplings[0][0].shape[3]
    majors, part, strip = parts[0].shape
    rows = part * ROW_CHUNKS // 2
    chunk = rows // pieces

    def spec(count):
        def block(i, ids, entries, *_):
            wanted = (ids[2] * 2 + ids[3]) ^ (base + i)
            return (entries[ids[0] * bands + wanted], 0, 0, 0)

        return pl.BlockSpec((1, count, chunk, tile), block)

    calls = bands // 2
    return pl.pallas_call(
        lambda *refs: product_kernel(groups, pieces, lanes, base, *refs),
        grid_spec=pltpu.PrefetchScalarGridSpec(
            num_scalar_prefetch=5,
            grid=(calls,),
            in_specs=[spec(count) for count in groups for _ in range(pieces)]
            + [pl.BlockSpec(memory_space=pltpu.HBM)] * len(parts),
            out_specs=[
                pl.BlockSpec((1, rows, strip), lambda i, *_: (i, 0, 0)),
                pl.BlockSpec((1, strip, rows), lambda i, *_: (i, 0, 0)),
            ],
            scratch_shapes=[
                pltpu.VMEM((len(parts) * majors * part, strip), jnp.bfloat16),
                pltpu.SemaphoreType.DMA((len(parts) * majors,)),
            ],
        ),
        out_shape=[
            jax.ShapeDtypeStruct((calls, rows, strip), jnp.float32),
            jax.ShapeDtypeStruct((calls, strip, rows), jnp.float32),
        ],
        compiler_params=pltpu.CompilerParams(vmem_limit_bytes=40 << 20),
        cost_estimate=pl.CostEstimate(
            flops=2 * calls * sum(groups) * rows * tile * strip,
            bytes_accessed=2 * (calls * sum(groups) * rows * tile + len(parts) * majors * part * strip),
            transcendentals=0,
        ),
    )(
        ids,
        entries,
        tile_cols.reshape(-1),
        tile_count,
        scale[None],
        *[piece for group in couplings for piece in group],
        *parts,
    )


def send_direct(grid, sigma, base):
    return [
        grid.send(
            sigma[i],
            lambda z, x, m, n: ((m * 2 + n) ^ (base + i), x, z // 2, z % 2),
            lambda z, x, m, n: (z, (x + 1) % grid.lanes, m, n),
        )
        for i in range(sigma.shape[0])
    ]


def bring_home(grid, run, ids, band, lane, major, minor):
    bands, lanes, majors = grid.bands, grid.lanes, grid.majors
    far, far_mirror = run(ids, bands // 2)
    far, far_mirror = far.astype(jnp.float16), far_mirror.astype(jnp.float16)
    received_far = send_direct(grid, far, bands // 2)
    entries = grid.send(far_mirror, lambda z, x, m, n: (z, x, m ^ (majors // 2), n))
    near, near_mirror = run(after(ids, far, far_mirror), 0)
    near, near_mirror = near.astype(jnp.float16), near_mirror.astype(jnp.float16)
    received = send_direct(grid, near, 0) + received_far

    entries = [near_mirror[i] for i in range(bands // 2)] + [entries[i] for i in range(bands // 2)]
    for bit in bits(majors)[1:]:
        moved = [j for j in range(bands) if j // 2 & bit]
        brought = grid.send(jnp.stack([entries[j] for j in moved]), lambda z, x, m, n: (z, x, m ^ bit, n))
        for i, j in enumerate(moved):
            entries[j] = brought[i]
    strip, part = entries[0].shape
    share = strip // lanes
    table = {}
    for turn in range(lanes):
        turned = [lax.dynamic_slice_in_dim(entry, (lane ^ turn) * share, share, 0) for entry in entries]
        turned = grid.send(jnp.stack(turned), lambda z, x, m, n: (z, x ^ turn, m, n))
        for j in range(bands):
            table[j, turn] = turned[j]
    moved = [(j, turn) for j in range(1, bands, 2) for turn in range(lanes)]
    brought = grid.send(jnp.stack([table[key] for key in moved]), lambda z, x, m, n: (z, x, m, 1 - n))
    for i, key in enumerate(moved):
        table[key] = brought[i]

    rows = 2 * part
    direct = jnp.zeros((rows, lanes * rows), jnp.float16)
    for key in range(majors):
        pair = jnp.concatenate(ordered(received[2 * key : 2 * key + 2], band % 2))
        for x in range(lanes):
            first = (x * majors + ((band // 2) ^ key)) * share
            direct = lax.dynamic_update_slice_in_dim(direct, pair[:, x * share : (x + 1) * share], first, 1)
    mirror = jnp.zeros((rows, lanes * rows), jnp.float16)
    for turn in range(lanes):
        for flip in range(2):
            block = jnp.concatenate(ordered([table[2 * key + flip, turn] for key in range(majors)], major))
            first = ((lane ^ turn) * 2 + (minor ^ flip)) * part
            mirror = lax.dynamic_update_slice_in_dim(mirror, block, first, 1)
    return direct, mirror


def body(coeffs, denominator, coupling, tile_cols, tile_count):
    rows = coeffs.shape[0]
    _, slots, tile = coupling.shape
    grid = Grid(lax.axis_size("alpha"), lax.axis_size("beta"))
    alpha, beta = lax.axis_index("alpha"), lax.axis_index("beta")
    band, lane = alpha // grid.lanes, alpha % grid.lanes
    major, minor = beta // 2, beta % 2
    ids = jnp.stack([band, lane, major, minor]).astype(jnp.int32)
    all_rows = (jnp.arange(grid.bands * grid.lanes) * rows // tile).reshape(grid.bands, grid.lanes)
    many = tile_count[all_rows] > slots // 2
    busy = jnp.take(many, lane, axis=1)

    def one_busy(*values):
        return spread_inputs(grid, *values, busy, band, lane, major, minor)

    def any_busy(*values):
        return spread_inputs(grid, *values, None, band, lane, major, minor)

    couplings, largest, parts = lax.cond(
        jnp.max(jnp.sum(many, axis=0)) <= 1, one_busy, any_busy, coupling, coeffs
    )
    entries = jnp.array([row.index(z) for row in line_order(grid.bands) for z in range(grid.bands)], jnp.int32)
    growth = slots * tile * COUPLING_MAX
    current = coeffs
    for step_index in range(STEPS):
        scale = HALF_TOP / (growth * largest)
        largest = largest * (1 + 2 * growth / DENOMINATOR_MIN)
        if step_index:
            half = current.astype(jnp.bfloat16)
            parts = to_columns(grid, half, band, lane, major, minor, [], [1, ROW_CHUNKS - 1], False)

        def run(ids, base):
            return products(grid, couplings, parts, ids, entries, tile_cols, tile_count, scale, base)

        direct, mirror = bring_home(grid, run, ids, band, lane, major, minor)
        total = (direct.astype(jnp.float32) + mirror.astype(jnp.float32)) / scale
        current = current - total / denominator
    return current


def solution(mesh):
    placed = (P("alpha", "beta"), P("alpha", "beta"), P("alpha", None, None), P(), P())
    return jax.shard_map(
        body, mesh=mesh, in_specs=placed, out_specs=P("alpha", "beta"), check_vma=False
    )
```

```python
import jax
import jax.numpy as jnp
from jax import lax
from jax.experimental import pallas as pl
from jax.experimental.pallas import tpu as pltpu
from jax.sharding import PartitionSpec as P

STEPS = 2
COUPLING_MAX = 0.15625
DENOMINATOR_MIN = 1.5
HALF_TOP = 60000.0
AXES = ("alpha", "beta")
ROW_CHUNKS = 4


class Grid:
    def __init__(self, alpha_devices, beta_devices):
        self.bands = beta_devices
        self.lanes = alpha_devices // beta_devices
        self.majors = beta_devices // 2
        self.places = [
            (band, lane, major, minor)
            for band in range(self.bands)
            for lane in range(self.lanes)
            for major in range(self.majors)
            for minor in range(2)
        ]

    def index(self, band, lane, major, minor):
        return ((band * self.lanes + lane) * self.majors + major) * 2 + minor

    def send(self, value, where, idle=None):
        stays = [where(*place) == place for place in self.places]
        if all(stays):
            return value
        pairs = []
        for place, stay in zip(self.places, stays):
            target = idle(*place) if stay else where(*place)
            pairs.append((self.index(*place), self.index(*target)))
        received = lax.ppermute(value, AXES, pairs)
        if any(stays):
            device = lax.axis_index("alpha") * self.bands + lax.axis_index("beta")
            received = jnp.where(jnp.array(stays)[device], value, received)
        return received


def after(value, *earlier):
    earlier = [array for array in earlier if array is not None]
    return lax.optimization_barrier((value, *earlier))[0] if earlier else value


def bits(count):
    return [1 << i for i in reversed(range(count.bit_length() - 1))]


def ordered(entries, me):
    if len(entries) == 1:
        return entries
    half = len(entries) // 2
    near, far = ordered(entries[:half], me), ordered(entries[half:], me)
    low = (me & half) == 0
    pairs = list(zip(near, far))
    return [jnp.where(low, a, b) for a, b in pairs] + [jnp.where(low, b, a) for a, b in pairs]


def line_order(bands):
    order, half = [[z] for z in range(bands)], 1
    while half < bands:
        middle = [z // (2 * half) * 2 * half + half - (z // half % 2) for z in range(bands)]
        order, half = [order[z] + order[middle[z]] for z in range(bands)], 2 * half
    return order


def gather_bands(grid, own, band, busy=None):
    held = own[None]
    brought = []
    width = 2
    while width <= grid.bands:
        half = width // 2
        moving, kept = held, None
        for hop in range(half):
            partner = list(range(grid.bands))
            for base in range(0, grid.bands, width):
                low, high = base + half - 1, base + half
                if hop == 0:
                    pairs = [(low, high)]
                else:
                    pairs = [(low - hop + 1, low - hop), (high + hop - 1, high + hop)]
                for one, other in pairs:
                    partner[one], partner[other] = other, one
            pairs = [
                (grid.index(z, x, m, n), grid.index(partner[z], x, m, 1 - n if partner[z] == z else n))
                for z, x, m, n in grid.places
            ]
            moving = lax.ppermute(moving, AXES, pairs)
            if hop == 0:
                brought.append(moving)
            takes = [(half - 1 - z % width if z % width < half else z % width - half) == hop for z in range(grid.bands)]
            kept = moving if kept is None else jnp.where(jnp.array(takes)[band], moving, kept)
        if busy is None:
            held = jnp.concatenate([held, kept])
        else:
            mine = jnp.any(busy & (jnp.arange(grid.bands) // half == band // half))
            held = jnp.where(mine, held, kept)
        width *= 2
    return held, brought


def spread_majors(grid, line):
    pieces = {0: line}
    for bit in bits(grid.majors):
        received = {key ^ bit: grid.send(piece, lambda z, x, m, n: (z, x, m ^ bit, n)) for key, piece in pieces.items()}
        pieces.update(received)
    return [pieces[key] for key in range(grid.majors)]


def spread_inputs(grid, coupling, coeffs, busy, band, lane, major, minor):
    rows, slots, tile = coupling.shape
    chunk = rows // (2 * grid.majors)
    first = (minor * grid.majors + major) * chunk
    dense = slots if busy is None else slots // 2
    groups = [(slot, 1) for slot in range(dense)]
    if busy is not None:
        groups.append((dense, slots - dense))
    rider = 1
    lines, gates = [], [None]
    half, extreme = None, None
    for number, (slot, count) in enumerate(groups):
        source = after(coupling, gates[-1])
        own = [lax.dynamic_slice(source, (first, slot + i, 0), (chunk, 1, tile)) for i in range(count)]
        own = jnp.concatenate([one.reshape(1, chunk, tile) for one in own])
        if number == 0:
            half = after(coeffs, own).astype(jnp.bfloat16)
            extreme = jnp.max(jnp.abs(lax.optimization_barrier(half))).astype(jnp.float32)
            extreme = (jnp.maximum(extreme, 1e-30) * 1.01).astype(jnp.bfloat16)
            extreme = jnp.full((16, tile), extreme)
        if number == rider:
            for where in (lambda z, x, m, n: (z, x, m, 1 - n), lambda z, x, m, n: (z, (x + 1) % grid.lanes, m, n)):
                extreme = jnp.maximum(extreme, grid.send(extreme, where))
            own = jnp.concatenate([own, jnp.broadcast_to(extreme, (count, *extreme.shape))], axis=1)
        line, brought = gather_bands(grid, own, band, None if slot < dense else busy)
        gates.append(brought[0])
        lines.append((line, brought))
    gathered = [spread_majors(grid, line) for line, _ in lines]
    rode = [piece[:, 0, chunk, 0] for piece in gathered[rider]]
    largest = jnp.max(jnp.stack(rode)).astype(jnp.float32)
    z_gates = [lines[0][0], lines[1][1][-1], gathered[0][-1], gathered[1][-1]]
    parts = to_columns(grid, half, band, lane, major, minor, z_gates, [ROW_CHUNKS], True)
    result = []
    for (slot, count), pieces in zip(groups, gathered):
        if slot >= dense:
            pieces = [jnp.broadcast_to(piece, (grid.bands, *piece.shape[1:])) for piece in pieces]
        if chunk % 16:
            whole = jnp.take(jnp.stack(pieces), major ^ jnp.arange(grid.majors), axis=0)[:, :, :, :chunk]
            pieces = [whole.transpose(1, 2, 0, 3, 4).reshape(grid.bands, count, rows // 2, tile)]
        result.append(pieces)
    if busy is None:
        late, result = result[dense // 2 :], result[: dense // 2]
        kept = rows // 2 // len(late[0])
        joined = [jnp.concatenate([one[:, :, :kept] for one in ones], axis=1) for ones in zip(*late)]
        result.append(joined)
    return result, largest, parts


def to_columns(grid, half, band, lane, major, minor, gates, batches, by_lane):
    rows = half.shape[0]
    lanes, majors = grid.lanes, grid.majors
    part, share = rows // ROW_CHUNKS, rows // majors

    def idle(z, x, m, n):
        return (z, (x + 1) % lanes, m, n) if by_lane else (z, x, m ^ 1, n)

    firsts, done = [], 0
    for batch in batches:
        block = half[done * part : (done + batch) * part]
        first = []
        for key in range(majors):
            piece = [
                lax.dynamic_slice_in_dim(block, (x * majors + (major ^ key)) * share, share, 1) for x in range(lanes)
            ]
            first.append(grid.send(jnp.concatenate(piece, 1), lambda z, x, m, n: (z, x, m ^ key, n)))
        firsts += [[one[i * part : (i + 1) * part] for one in first] for i in range(batch)]
        done += batch
    parts, earlier = [], [None] * majors
    for chunk, first in enumerate(firsts):
        first = jnp.stack(first)
        second = []
        for key in range(majors):
            piece = lax.dynamic_index_in_dim(first, (band // 2) ^ key ^ major, 0, keepdims=False)
            piece = after(piece, earlier[key], gates[min(chunk, len(gates) - 1)] if gates else None)
            piece = grid.send(piece, lambda z, x, m, n: ((z // 2 ^ key) * 2 + n, x, m, z % 2), idle)
            earlier[key] = piece
            second.append(piece)
        second = jnp.stack(second)
        for turn in range(lanes):
            third = grid.send(second, lambda z, x, m, n: (z, (x + turn) % lanes, m, n))
            parts += [third, grid.send(third, lambda z, x, m, n: (z, x, m, 1 - n))]
    return parts


def product_kernel(groups, pieces, lanes, base, id_ref, entry_ref, column_ref, count_ref, scale_ref, *refs):
    couplings, parts = refs[: len(groups) * pieces], refs[len(groups) * pieces : -4]
    out_ref, mirror_ref, coeff_ref, sems = refs[-4:]
    band, lane, major, minor = (id_ref[i] for i in range(4))
    chunk = out_ref.shape[1] // pieces
    tile = couplings[0].shape[3]
    majors, part, _ = parts[0].shape
    bands, rows = 2 * majors, part * ROW_CHUNKS
    wanted = (major * 2 + minor) ^ (2 * pl.program_id(0) + base)
    tile_row = (wanted * lanes + lane) * rows // tile

    @pl.when(pl.program_id(0) == 0)
    def _():
        copies = []
        for i, ref in enumerate(parts):
            turn, flip = i // 2 % lanes, i % 2
            for key in range(majors):
                alpha = (((band // 2) ^ key) * 2 + (minor ^ flip)) * lanes + lax.rem(lane + lanes - turn, lanes)
                first = pl.multiple_of(alpha * rows + i // (2 * lanes) * part, part)
                target = coeff_ref.at[pl.ds(first, part)]
                copies.append(pltpu.make_async_copy(ref.at[key], target, sems.at[i * majors + key]))
        for copy in copies:
            copy.start()
        for copy in copies:
            copy.wait()

    def product(number, i, slot):
        first = pl.multiple_of(column_ref[tile_row * sum(groups) + slot] * tile, tile)
        left = [couplings[number * pieces + piece][0, i, :chunk] for piece in range(pieces)]
        left = jnp.concatenate(left, axis=0)
        return jnp.dot(left, coeff_ref[pl.ds(first, tile), :], preferred_element_type=jnp.float32) * scale_ref[0]

    def store(value, add):
        for piece in range(pieces):
            first = (major ^ piece) * chunk if pieces > 1 else 0
            place = pl.ds(pl.multiple_of(first, chunk), chunk)
            rows_of = value[piece * chunk : (piece + 1) * chunk]
            out_ref[0, place, :] = out_ref[0, place, :] + rows_of if add else rows_of

    slot = 0
    for number, count in enumerate(groups):
        for i in range(count):
            if slot == 0:
                store(product(number, i, slot), False)
            else:
                pl.when(slot < count_ref[tile_row])(lambda: store(product(number, i, slot), True))
            slot += 1

    mirror_ref[0] = out_ref[0].T


def products(grid, couplings, parts, ids, entries, tile_cols, tile_count, scale, base):
    bands, lanes = grid.bands, grid.lanes
    groups, pieces = [group[0].shape[1] for group in couplings], len(couplings[0])
    tile = couplings[0][0].shape[3]
    majors, part, strip = parts[0].shape
    rows = part * ROW_CHUNKS // 2
    chunk = rows // pieces

    def spec(count):
        def block(i, ids, entries, *_):
            wanted = (ids[2] * 2 + ids[3]) ^ (2 * i + base)
            return (entries[ids[0] * bands + wanted], 0, 0, 0)

        return pl.BlockSpec((1, count, chunk, tile), block)

    calls = bands // 2
    return pl.pallas_call(
        lambda *refs: product_kernel(groups, pieces, lanes, base, *refs),
        grid_spec=pltpu.PrefetchScalarGridSpec(
            num_scalar_prefetch=5,
            grid=(calls,),
            in_specs=[spec(count) for count in groups for _ in range(pieces)]
            + [pl.BlockSpec(memory_space=pltpu.HBM)] * len(parts),
            out_specs=[
                pl.BlockSpec((1, rows, strip), lambda i, *_: (i, 0, 0)),
                pl.BlockSpec((1, strip, rows), lambda i, *_: (i, 0, 0)),
            ],
            scratch_shapes=[
                pltpu.VMEM((len(parts) * majors * part, strip), jnp.bfloat16),
                pltpu.SemaphoreType.DMA((len(parts) * majors,)),
            ],
        ),
        out_shape=[
            jax.ShapeDtypeStruct((calls, rows, strip), jnp.float32),
            jax.ShapeDtypeStruct((calls, strip, rows), jnp.float32),
        ],
        compiler_params=pltpu.CompilerParams(vmem_limit_bytes=40 << 20),
        cost_estimate=pl.CostEstimate(
            flops=2 * calls * sum(groups) * rows * tile * strip,
            bytes_accessed=2 * (calls * sum(groups) * rows * tile + len(parts) * majors * part * strip),
            transcendentals=0,
        ),
    )(
        ids,
        entries,
        tile_cols.reshape(-1),
        tile_count,
        scale[None],
        *[piece for group in couplings for piece in group],
        *parts,
    )


def bring_home(grid, run, ids, band, lane, major, minor):
    bands, lanes, majors = grid.bands, grid.lanes, grid.majors
    received, table, gate = [None] * bands, {}, []
    for base in range(2):
        sigma, mirrored = run(after(ids, gate), base)
        sigma, mirrored = sigma.astype(jnp.float16), mirrored.astype(jnp.float16)
        gate = [sigma, mirrored]
        if base:
            sigma, mirrored = after((sigma, mirrored), received[0::2])
        strip, part = mirrored.shape[1:]
        share = strip // lanes
        for i in range(majors):
            key = 2 * i + base
            received[key] = grid.send(
                sigma[i],
                lambda z, x, m, n: ((m * 2 + n) ^ key, x, z // 2, z % 2),
                lambda z, x, m, n: (z, (x + 1) % lanes, m, n),
            )
            for turn in range(lanes):
                piece = lax.dynamic_slice_in_dim(mirrored[i], (lane ^ turn) * share, share, 0)
                table[key, turn] = grid.send(piece, lambda z, x, m, n: (z, x ^ turn, m ^ i, n ^ base))

    rows = 2 * part
    direct = jnp.zeros((rows, lanes * rows), jnp.float16)
    for key in range(majors):
        pair = jnp.concatenate(ordered(received[2 * key : 2 * key + 2], band % 2))
        for x in range(lanes):
            first = (x * majors + ((band // 2) ^ key)) * share
            direct = lax.dynamic_update_slice_in_dim(direct, pair[:, x * share : (x + 1) * share], first, 1)
    mirror = jnp.zeros((rows, lanes * rows), jnp.float16)
    for turn in range(lanes):
        for flip in range(2):
            block = jnp.concatenate(ordered([table[2 * key + flip, turn] for key in range(majors)], major))
            first = ((lane ^ turn) * 2 + (minor ^ flip)) * part
            mirror = lax.dynamic_update_slice_in_dim(mirror, block, first, 1)
    return direct, mirror


def body(coeffs, denominator, coupling, tile_cols, tile_count):
    rows = coeffs.shape[0]
    _, slots, tile = coupling.shape
    grid = Grid(lax.axis_size("alpha"), lax.axis_size("beta"))
    alpha, beta = lax.axis_index("alpha"), lax.axis_index("beta")
    band, lane = alpha // grid.lanes, alpha % grid.lanes
    major, minor = beta // 2, beta % 2
    ids = jnp.stack([band, lane, major, minor]).astype(jnp.int32)
    all_rows = (jnp.arange(grid.bands * grid.lanes) * rows // tile).reshape(grid.bands, grid.lanes)
    many = tile_count[all_rows] > slots // 2
    busy = jnp.take(many, lane, axis=1)

    def one_busy(*values):
        return spread_inputs(grid, *values, busy, band, lane, major, minor)

    def any_busy(*values):
        return spread_inputs(grid, *values, None, band, lane, major, minor)

    couplings, largest, parts = lax.cond(
        jnp.max(jnp.sum(many, axis=0)) <= 1, one_busy, any_busy, coupling, coeffs
    )
    entries = jnp.array([row.index(z) for row in line_order(grid.bands) for z in range(grid.bands)], jnp.int32)
    growth = slots * tile * COUPLING_MAX
    current = coeffs
    for step_index in range(STEPS):
        scale = HALF_TOP / (growth * largest)
        largest = largest * (1 + 2 * growth / DENOMINATOR_MIN)
        if step_index:
            half = current.astype(jnp.bfloat16)
            parts = to_columns(grid, half, band, lane, major, minor, [], [ROW_CHUNKS // 2] * 2, False)

        def run(ids, base):
            return products(grid, couplings, parts, ids, entries, tile_cols, tile_count, scale, base)

        direct, mirror = bring_home(grid, run, ids, band, lane, major, minor)
        total = (direct.astype(jnp.float32) + mirror.astype(jnp.float32)) / scale
        current = current - total / denominator
    return current


def solution(mesh):
    placed = (P("alpha", "beta"), P("alpha", "beta"), P("alpha", None, None), P(), P())
    return jax.shard_map(
        body, mesh=mesh, in_specs=placed, out_specs=P("alpha", "beta"), check_vma=False
    )
```

```python
import functools

import jax
import jax.numpy as jnp
from jax import lax
from jax.experimental import pallas as pl
from jax.experimental.pallas import tpu as pltpu
from jax.sharding import PartitionSpec as P

STEPS = 2
COUPLING_MAX = 0.15625
DENOMINATOR_MIN = 1.5
HALF_TOP = 60000.0
AXES = ("alpha", "beta")
ROW_CHUNKS = 4


class Grid:
    def __init__(self, alpha_devices, beta_devices):
        self.bands = beta_devices
        self.lanes = alpha_devices // beta_devices
        self.majors = beta_devices // 2
        self.places = [
            (band, lane, major, minor)
            for band in range(self.bands)
            for lane in range(self.lanes)
            for major in range(self.majors)
            for minor in range(2)
        ]

    def index(self, band, lane, major, minor):
        return ((band * self.lanes + lane) * self.majors + major) * 2 + minor

    def send(self, value, where, idle=None, arrivals=None):
        stays = [where(*place) == place for place in self.places]
        if all(stays):
            return value
        pairs = []
        for place, stay in zip(self.places, stays):
            target = idle(*place) if stay else where(*place)
            pairs.append((self.index(*place), self.index(*target)))
        received = lax.ppermute(value, AXES, pairs)
        if arrivals is not None:
            arrivals.append(received)
        if any(stays):
            device = lax.axis_index("alpha") * self.bands + lax.axis_index("beta")
            received = jnp.where(jnp.array(stays)[device], value, received)
        return received


def after(value, *earlier):
    earlier = jax.tree.leaves(earlier)
    return lax.optimization_barrier((value, *earlier))[0] if earlier else value


def bits(count):
    return [1 << i for i in reversed(range(count.bit_length() - 1))]


def ordered(entries, me):
    if len(entries) == 1:
        return entries
    half = len(entries) // 2
    near, far = ordered(entries[:half], me), ordered(entries[half:], me)
    low = (me & half) == 0
    pairs = list(zip(near, far))
    return [jnp.where(low, a, b) for a, b in pairs] + [jnp.where(low, b, a) for a, b in pairs]


def line_order(bands):
    order, half = [[z] for z in range(bands)], 1
    while half < bands:
        middle = [z // (2 * half) * 2 * half + half - (z // half % 2) for z in range(bands)]
        order, half = [order[z] + order[middle[z]] for z in range(bands)], 2 * half
    return order


def gather_bands(grid, own, band, busy=None):
    held = own[None]
    brought = []
    width = 2
    while width <= grid.bands:
        half = width // 2
        moving, kept = held, None
        for hop in range(half):
            partner = list(range(grid.bands))
            for base in range(0, grid.bands, width):
                low, high = base + half - 1, base + half
                if hop == 0:
                    pairs = [(low, high)]
                else:
                    pairs = [(low - hop + 1, low - hop), (high + hop - 1, high + hop)]
                for one, other in pairs:
                    partner[one], partner[other] = other, one
            pairs = [
                (grid.index(z, x, m, n), grid.index(partner[z], x, m, 1 - n if partner[z] == z else n))
                for z, x, m, n in grid.places
            ]
            moving = lax.ppermute(moving, AXES, pairs)
            if hop == 0:
                brought.append(moving)
            takes = [(half - 1 - z % width if z % width < half else z % width - half) == hop for z in range(grid.bands)]
            kept = moving if kept is None else jnp.where(jnp.array(takes)[band], moving, kept)
        if busy is None:
            held = jnp.concatenate([held, kept])
        else:
            mine = jnp.any(busy & (jnp.arange(grid.bands) // half == band // half))
            held = jnp.where(mine, held, kept)
        width *= 2
    return held, brought


def spread_majors(grid, line):
    pieces = {0: line}
    for bit in bits(grid.majors):
        received = {key ^ bit: grid.send(piece, lambda z, x, m, n: (z, x, m ^ bit, n)) for key, piece in pieces.items()}
        pieces.update(received)
    return [pieces[key] for key in range(grid.majors)]


def spread_inputs(grid, coupling, coeffs, busy, band, lane, major, minor):
    rows, slots, tile = coupling.shape
    chunk = rows // (2 * grid.majors)
    first = (minor * grid.majors + major) * chunk
    dense = slots if busy is None else slots // 2
    groups = [(slot, 1) for slot in range(dense)]
    if busy is not None:
        groups.append((dense, slots - dense))
    rider = 1
    lines, gates = [], [None]
    half, extreme = None, None
    for number, (slot, count) in enumerate(groups):
        source = after(coupling, gates[-1])
        own = [lax.dynamic_slice(source, (first, slot + i, 0), (chunk, 1, tile)) for i in range(count)]
        own = jnp.concatenate([one.reshape(1, chunk, tile) for one in own])
        if number == 0:
            half = after(coeffs, own).astype(jnp.bfloat16)
            extreme = jnp.max(jnp.abs(lax.optimization_barrier(half))).astype(jnp.float32)
            extreme = (jnp.maximum(extreme, 1e-30) * 1.01).astype(jnp.bfloat16)
            extreme = jnp.full((16, tile), extreme)
        if number == rider:
            for where in (lambda z, x, m, n: (z, x, m, 1 - n), lambda z, x, m, n: (z, (x + 1) % grid.lanes, m, n)):
                extreme = jnp.maximum(extreme, grid.send(extreme, where))
            own = jnp.concatenate([own, jnp.broadcast_to(extreme, (count, *extreme.shape))], axis=1)
        line, brought = gather_bands(grid, own, band, None if slot < dense else busy)
        gates.append(brought[0])
        lines.append((line, brought))
    gathered = [spread_majors(grid, line) for line, _ in lines]
    rode = [piece[:, 0, chunk, 0] for piece in gathered[rider]]
    largest = jnp.max(jnp.stack(rode)).astype(jnp.float32)
    z_gates = [lines[0][0], lines[1][1][-1], gathered[0][-1], gathered[1][-1]]
    parts = to_columns(grid, half, band, lane, major, minor, z_gates, [ROW_CHUNKS], True)
    result = []
    for (slot, count), pieces in zip(groups, gathered):
        if slot >= dense:
            pieces = [jnp.broadcast_to(piece, (grid.bands, *piece.shape[1:])) for piece in pieces]
        if chunk % 16:
            whole = jnp.take(jnp.stack(pieces), major ^ jnp.arange(grid.majors), axis=0)[:, :, :, :chunk]
            pieces = [whole.transpose(1, 2, 0, 3, 4).reshape(grid.bands, count, rows // 2, tile)]
        result.append(pieces)
    if busy is None:
        late, result = result[dense // 2 :], result[: dense // 2]
        kept = rows // 2 // len(late[0])
        joined = [jnp.concatenate([one[:, :, :kept] for one in ones], axis=1) for ones in zip(*late)]
        result.append(joined)
    return result, largest, parts


def to_columns(grid, half, band, lane, major, minor, gates, batches, by_lane):
    rows = half.shape[0]
    lanes, majors = grid.lanes, grid.majors
    part, share = rows // ROW_CHUNKS, rows // majors

    def idle(z, x, m, n):
        return (z, (x + 1) % lanes, m, n) if by_lane else (z, x, m ^ 1, n)

    firsts, done = [], 0
    for batch in batches:
        block = half[done * part : (done + batch) * part]
        first = []
        for key in range(majors):
            piece = [
                lax.dynamic_slice_in_dim(block, (x * majors + (major ^ key)) * share, share, 1) for x in range(lanes)
            ]
            first.append(grid.send(jnp.concatenate(piece, 1), lambda z, x, m, n: (z, x, m ^ key, n)))
        firsts += [[one[i * part : (i + 1) * part] for one in first] for i in range(batch)]
        done += batch
    parts, earlier = [], [None] * majors
    for chunk, first in enumerate(firsts):
        first = jnp.stack(first)
        second = []
        for key in range(majors):
            piece = lax.dynamic_index_in_dim(first, (band // 2) ^ key ^ major, 0, keepdims=False)
            piece = after(piece, earlier[key], gates[min(chunk, len(gates) - 1)] if gates else None)
            piece = grid.send(piece, lambda z, x, m, n: ((z // 2 ^ key) * 2 + n, x, m, z % 2), idle)
            earlier[key] = piece
            second.append(piece)
        second = jnp.stack(second)
        for turn in range(lanes):
            third = grid.send(second, lambda z, x, m, n: (z, (x + turn) % lanes, m, n))
            parts += [third, grid.send(third, lambda z, x, m, n: (z, x, m, 1 - n))]
    return parts


def product_kernel(groups, pieces, lanes, out_calls, base, id_ref, entry_ref, column_ref, count_ref, scale_ref, *refs):
    couplings, parts = refs[: len(groups) * pieces], refs[len(groups) * pieces : -4]
    out_ref, mirror_ref, coeff_ref, sems = refs[-4:]
    band, lane, major, minor = (id_ref[i] for i in range(4))
    chunk = out_ref.shape[1] // pieces
    tile = couplings[0].shape[3]
    majors, part, _ = parts[0].shape
    bands, rows = 2 * majors, part * ROW_CHUNKS
    wanted = (major * 2 + minor) ^ (2 * pl.program_id(0) + base)
    tile_row = (wanted * lanes + lane) * rows // tile

    @pl.when(pl.program_id(0) == 0)
    def _():
        wanted_rows = [
            (((major * 2 + minor) ^ (2 * i + base)) * lanes + lane) * rows // tile for i in range(out_calls)
        ]
        used = [
            (column_ref[row * sum(groups) + slot], slot < count_ref[row])
            for row in wanted_rows
            for slot in range(sum(groups))
        ]
        copies = []
        for i in range(2 * lanes):
            turn, flip = i // 2, i % 2
            for key in range(majors):
                alpha = (((band // 2) ^ key) * 2 + (minor ^ flip)) * lanes + lax.rem(lane + lanes - turn, lanes)
                column = alpha * rows // tile
                needed = functools.reduce(jnp.logical_or, [(one == column) & filled for one, filled in used])
                for number in range(i, len(parts), 2 * lanes):
                    first = pl.multiple_of(alpha * rows + number // (2 * lanes) * part, part)
                    target = coeff_ref.at[pl.ds(first, part)]
                    source = parts[number].at[key]
                    copies.append((needed, pltpu.make_async_copy(source, target, sems.at[number * majors + key])))
        for needed, copy in copies:
            pl.when(needed)(copy.start)
        for needed, copy in copies:
            pl.when(needed)(copy.wait)

    def product(number, i, slot):
        first = pl.multiple_of(column_ref[tile_row * sum(groups) + slot] * tile, tile)
        left = [couplings[number * pieces + piece][0, i, :chunk] for piece in range(pieces)]
        left = jnp.concatenate(left, axis=0)
        return jnp.dot(left, coeff_ref[pl.ds(first, tile), :], preferred_element_type=jnp.float32) * scale_ref[0]

    def store(value, add):
        for piece in range(pieces):
            first = (major ^ piece) * chunk if pieces > 1 else 0
            place = pl.ds(pl.multiple_of(first, chunk), chunk)
            rows_of = value[piece * chunk : (piece + 1) * chunk]
            out_ref[0, place, :] = out_ref[0, place, :] + rows_of if add else rows_of

    slot = 0
    for number, count in enumerate(groups):
        for i in range(count):
            if slot == 0:
                store(product(number, i, slot), False)
            else:
                pl.when(slot < count_ref[tile_row])(lambda: store(product(number, i, slot), True))
            slot += 1

    mirror_ref[0] = out_ref[0].T


def products(grid, couplings, parts, ids, entries, tile_cols, tile_count, scale, base):
    bands, lanes = grid.bands, grid.lanes
    groups, pieces = [group[0].shape[1] for group in couplings], len(couplings[0])
    tile = couplings[0][0].shape[3]
    majors, part, strip = parts[0].shape
    rows = part * ROW_CHUNKS // 2
    chunk = rows // pieces

    def spec(count):
        def block(i, ids, entries, *_):
            wanted = (ids[2] * 2 + ids[3]) ^ (2 * i + base)
            return (entries[ids[0] * bands + wanted], 0, 0, 0)

        return pl.BlockSpec((1, count, chunk, tile), block)

    calls = bands // 2
    return pl.pallas_call(
        lambda *refs: product_kernel(groups, pieces, lanes, calls, base, *refs),
        grid_spec=pltpu.PrefetchScalarGridSpec(
            num_scalar_prefetch=5,
            grid=(calls,),
            in_specs=[spec(count) for count in groups for _ in range(pieces)]
            + [pl.BlockSpec(memory_space=pltpu.HBM)] * len(parts),
            out_specs=[
                pl.BlockSpec((1, rows, strip), lambda i, *_: (i, 0, 0)),
                pl.BlockSpec((1, strip, rows), lambda i, *_: (i, 0, 0)),
            ],
            scratch_shapes=[
                pltpu.VMEM((len(parts) * majors * part, strip), jnp.bfloat16),
                pltpu.SemaphoreType.DMA((len(parts) * majors,)),
            ],
        ),
        out_shape=[
            jax.ShapeDtypeStruct((calls, rows, strip), jnp.float32),
            jax.ShapeDtypeStruct((calls, strip, rows), jnp.float32),
        ],
        compiler_params=pltpu.CompilerParams(vmem_limit_bytes=40 << 20),
        cost_estimate=pl.CostEstimate(
            flops=2 * calls * sum(groups) * rows * tile * strip,
            bytes_accessed=2 * (calls * sum(groups) * rows * tile + len(parts) * majors * part * strip),
            transcendentals=0,
        ),
    )(
        ids,
        entries,
        tile_cols.reshape(-1),
        tile_count,
        scale[None],
        *[piece for group in couplings for piece in group],
        *parts,
    )


def bring_home(grid, run, ids, band, lane, major, minor):
    bands, lanes, majors = grid.bands, grid.lanes, grid.majors
    received, table, gate, arrivals = [None] * bands, {}, [], []
    for base in range(2):
        sigma, mirrored = run(after(ids, gate), base)
        strip, part = mirrored.shape[1:]
        share = strip // lanes
        sigma, mirrored = sigma.astype(jnp.float16), mirrored.astype(jnp.float16)
        gate = [sigma, mirrored]
        if base:
            sigma, mirrored = after((sigma, mirrored), arrivals)
        for i in range(majors):
            key = 2 * i + base
            received[key] = grid.send(
                sigma[i],
                lambda z, x, m, n: ((m * 2 + n) ^ key, x, z // 2, z % 2),
                lambda z, x, m, n: (z, (x + 1) % lanes, m, n),
                None if base else arrivals,
            )
            for turn in range(lanes):
                piece = lax.dynamic_slice_in_dim(mirrored[i], (lane ^ turn) * share, share, 0)
                table[key, turn] = grid.send(piece, lambda z, x, m, n: (z, x ^ turn, m ^ i, n ^ base))

    rows = 2 * part
    direct = jnp.zeros((rows, lanes * rows), jnp.float16)
    for key in range(majors):
        pair = jnp.concatenate(ordered(received[2 * key : 2 * key + 2], band % 2))
        for x in range(lanes):
            first = (x * majors + ((band // 2) ^ key)) * share
            direct = lax.dynamic_update_slice_in_dim(direct, pair[:, x * share : (x + 1) * share], first, 1)
    mirror = jnp.zeros((rows, lanes * rows), jnp.float16)
    for turn in range(lanes):
        for flip in range(2):
            block = jnp.concatenate(ordered([table[2 * key + flip, turn] for key in range(majors)], major))
            first = ((lane ^ turn) * 2 + (minor ^ flip)) * part
            mirror = lax.dynamic_update_slice_in_dim(mirror, block, first, 1)
    return direct, mirror


def body(coeffs, denominator, coupling, tile_cols, tile_count):
    rows = coeffs.shape[0]
    _, slots, tile = coupling.shape
    grid = Grid(lax.axis_size("alpha"), lax.axis_size("beta"))
    alpha, beta = lax.axis_index("alpha"), lax.axis_index("beta")
    band, lane = alpha // grid.lanes, alpha % grid.lanes
    major, minor = beta // 2, beta % 2
    ids = jnp.stack([band, lane, major, minor]).astype(jnp.int32)
    all_rows = (jnp.arange(grid.bands * grid.lanes) * rows // tile).reshape(grid.bands, grid.lanes)
    many = tile_count[all_rows] > slots // 2
    busy = jnp.take(many, lane, axis=1)

    def one_busy(*values):
        return spread_inputs(grid, *values, busy, band, lane, major, minor)

    def any_busy(*values):
        return spread_inputs(grid, *values, None, band, lane, major, minor)

    couplings, largest, parts = lax.cond(
        jnp.max(jnp.sum(many, axis=0)) <= 1, one_busy, any_busy, coupling, coeffs
    )
    entries = jnp.array([row.index(z) for row in line_order(grid.bands) for z in range(grid.bands)], jnp.int32)
    growth = slots * tile * COUPLING_MAX
    current = coeffs
    for step_index in range(STEPS):
        scale = HALF_TOP / (growth * largest)
        largest = largest * (1 + 2 * growth / DENOMINATOR_MIN)
        if step_index:
            half = current.astype(jnp.bfloat16)
            parts = to_columns(grid, half, band, lane, major, minor, [], [ROW_CHUNKS // 2] * 2, False)

        def run(ids, base):
            return products(grid, couplings, parts, ids, entries, tile_cols, tile_count, scale, base)

        direct, mirror = bring_home(grid, run, ids, band, lane, major, minor)
        total = (direct.astype(jnp.float32) + mirror.astype(jnp.float32)) / scale
        current = current - total / denominator
    return current


def solution(mesh):
    placed = (P("alpha", "beta"), P("alpha", "beta"), P("alpha", None, None), P(), P())
    return jax.shard_map(
        body, mesh=mesh, in_specs=placed, out_specs=P("alpha", "beta"), check_vma=False
    )
```

```python
import functools

import jax
import jax.numpy as jnp
from jax import lax
from jax.experimental import pallas as pl
from jax.experimental.pallas import tpu as pltpu
from jax.sharding import PartitionSpec as P

STEPS = 2
COUPLING_MAX = 0.15625
DENOMINATOR_MIN = 1.5
HALF_TOP = 60000.0
AXES = ("alpha", "beta")
ROW_CHUNKS = 4


class Grid:
    def __init__(self, alpha_devices, beta_devices):
        self.bands = beta_devices
        self.lanes = alpha_devices // beta_devices
        self.majors = beta_devices // 2
        self.places = [
            (band, lane, major, minor)
            for band in range(self.bands)
            for lane in range(self.lanes)
            for major in range(self.majors)
            for minor in range(2)
        ]

    def index(self, band, lane, major, minor):
        return ((band * self.lanes + lane) * self.majors + major) * 2 + minor

    def send(self, value, where, idle=None, arrivals=None):
        stays = [where(*place) == place for place in self.places]
        if all(stays):
            return value
        pairs = []
        for place, stay in zip(self.places, stays):
            target = idle(*place) if stay else where(*place)
            pairs.append((self.index(*place), self.index(*target)))
        received = lax.ppermute(value, AXES, pairs)
        if arrivals is not None:
            arrivals.append(received)
        if any(stays):
            device = lax.axis_index("alpha") * self.bands + lax.axis_index("beta")
            received = jnp.where(jnp.array(stays)[device], value, received)
        return received


def after(value, *earlier):
    earlier = jax.tree.leaves(earlier)
    return lax.optimization_barrier((value, *earlier))[0] if earlier else value


def bits(count):
    return [1 << i for i in reversed(range(count.bit_length() - 1))]


def ordered(entries, me):
    if len(entries) == 1:
        return entries
    half = len(entries) // 2
    near, far = ordered(entries[:half], me), ordered(entries[half:], me)
    low = (me & half) == 0
    pairs = list(zip(near, far))
    return [jnp.where(low, a, b) for a, b in pairs] + [jnp.where(low, b, a) for a, b in pairs]


def line_order(bands):
    order, half = [[z] for z in range(bands)], 1
    while half < bands:
        middle = [z // (2 * half) * 2 * half + half - (z // half % 2) for z in range(bands)]
        order, half = [order[z] + order[middle[z]] for z in range(bands)], 2 * half
    return order


def gather_bands(grid, own, band, busy=None):
    held = own[None]
    brought = []
    width = 2
    while width <= grid.bands:
        half = width // 2
        moving, kept = held, None
        for hop in range(half):
            partner = list(range(grid.bands))
            for base in range(0, grid.bands, width):
                low, high = base + half - 1, base + half
                if hop == 0:
                    pairs = [(low, high)]
                else:
                    pairs = [(low - hop + 1, low - hop), (high + hop - 1, high + hop)]
                for one, other in pairs:
                    partner[one], partner[other] = other, one
            pairs = [
                (grid.index(z, x, m, n), grid.index(partner[z], x, m, 1 - n if partner[z] == z else n))
                for z, x, m, n in grid.places
            ]
            moving = lax.ppermute(moving, AXES, pairs)
            if hop == 0:
                brought.append(moving)
            takes = [(half - 1 - z % width if z % width < half else z % width - half) == hop for z in range(grid.bands)]
            kept = moving if kept is None else jnp.where(jnp.array(takes)[band], moving, kept)
        if busy is None:
            held = jnp.concatenate([held, kept])
        else:
            mine = jnp.any(busy & (jnp.arange(grid.bands) // half == band // half))
            held = jnp.where(mine, held, kept)
        width *= 2
    return held, brought


def spread_majors(grid, line):
    pieces = {0: line}
    for bit in bits(grid.majors):
        received = {key ^ bit: grid.send(piece, lambda z, x, m, n: (z, x, m ^ bit, n)) for key, piece in pieces.items()}
        pieces.update(received)
    return [pieces[key] for key in range(grid.majors)]


def spread_inputs(grid, coupling, coeffs, busy, band, lane, major, minor):
    rows, slots, tile = coupling.shape
    chunk = rows // (2 * grid.majors)
    first = (minor * grid.majors + major) * chunk
    dense = slots if busy is None else slots // 2
    groups = [(slot, 1) for slot in range(dense)]
    if busy is not None:
        groups.append((dense, slots - dense))
    rider = 1
    lines, gates = [], [None]
    half, extreme = None, None
    for number, (slot, count) in enumerate(groups):
        source = after(coupling, gates[-1])
        own = [lax.dynamic_slice(source, (first, slot + i, 0), (chunk, 1, tile)) for i in range(count)]
        own = jnp.concatenate([one.reshape(1, chunk, tile) for one in own])
        if number == 0:
            half = after(coeffs, own).astype(jnp.bfloat16)
            extreme = jnp.max(jnp.abs(lax.optimization_barrier(half))).astype(jnp.float32)
            extreme = (jnp.maximum(extreme, 1e-30) * 1.01).astype(jnp.bfloat16)
            extreme = jnp.full((16, tile), extreme)
        if number == rider:
            for where in (lambda z, x, m, n: (z, x, m, 1 - n), lambda z, x, m, n: (z, (x + 1) % grid.lanes, m, n)):
                extreme = jnp.maximum(extreme, grid.send(extreme, where))
            own = jnp.concatenate([own, jnp.broadcast_to(extreme, (count, *extreme.shape))], axis=1)
        line, brought = gather_bands(grid, own, band, None if slot < dense else busy)
        gates.append(brought[0])
        lines.append((line, brought))
    gathered = [spread_majors(grid, line) for line, _ in lines]
    rode = [piece[:, 0, chunk, 0] for piece in gathered[rider]]
    largest = jnp.max(jnp.stack(rode)).astype(jnp.float32)
    z_gates = [lines[0][0], lines[1][1][-1], gathered[0][-1], gathered[1][-1]]
    parts = to_columns(grid, half, band, lane, major, minor, z_gates, [ROW_CHUNKS], True)
    result = []
    for (slot, count), pieces in zip(groups, gathered):
        if slot >= dense:
            pieces = [jnp.broadcast_to(piece, (grid.bands, *piece.shape[1:])) for piece in pieces]
        if chunk % 16:
            whole = jnp.take(jnp.stack(pieces), major ^ jnp.arange(grid.majors), axis=0)[:, :, :, :chunk]
            pieces = [whole.transpose(1, 2, 0, 3, 4).reshape(grid.bands, count, rows // 2, tile)]
        result.append(pieces)
    if busy is None:
        late, result = result[dense // 2 :], result[: dense // 2]
        kept = rows // 2 // len(late[0])
        joined = [jnp.concatenate([one[:, :, :kept] for one in ones], axis=1) for ones in zip(*late)]
        result.append(joined)
    return result, largest, parts


def to_columns(grid, half, band, lane, major, minor, gates, batches, by_lane):
    rows = half.shape[0]
    lanes, majors = grid.lanes, grid.majors
    part, share = rows // ROW_CHUNKS, rows // majors

    def idle(z, x, m, n):
        return (z, (x + 1) % lanes, m, n) if by_lane else (z, x, m ^ 1, n)

    firsts, done = [], 0
    for batch in batches:
        block = half[done * part : (done + batch) * part]
        first = []
        for key in range(majors):
            piece = [
                lax.dynamic_slice_in_dim(block, (x * majors + (major ^ key)) * share, share, 1) for x in range(lanes)
            ]
            first.append(grid.send(jnp.concatenate(piece, 1), lambda z, x, m, n: (z, x, m ^ key, n)))
        firsts += [[one[i * part : (i + 1) * part] for one in first] for i in range(batch)]
        done += batch
    parts, earlier = [], [None] * majors
    for chunk, first in enumerate(firsts):
        first = jnp.stack(first)
        second = []
        for key in range(majors):
            piece = lax.dynamic_index_in_dim(first, (band // 2) ^ key ^ major, 0, keepdims=False)
            piece = after(piece, earlier[key], gates[min(chunk, len(gates) - 1)] if gates else None)
            piece = grid.send(piece, lambda z, x, m, n: ((z // 2 ^ key) * 2 + n, x, m, z % 2), idle)
            earlier[key] = piece
            second.append(piece)
        second = jnp.stack(second)
        for turn in range(lanes):
            third = grid.send(second, lambda z, x, m, n: (z, (x + turn) % lanes, m, n))
            parts += [third, grid.send(third, lambda z, x, m, n: (z, x, m, 1 - n))]
    return parts


def product_kernel(groups, pieces, lanes, out_calls, base, id_ref, entry_ref, column_ref, count_ref, scale_ref, *refs):
    couplings, parts = refs[: len(groups) * pieces], refs[len(groups) * pieces : -4]
    out_ref, mirror_ref, coeff_ref, sems = refs[-4:]
    band, lane, major, minor = (id_ref[i] for i in range(4))
    chunk = out_ref.shape[1] // pieces
    tile = couplings[0].shape[3]
    majors, part, _ = parts[0].shape
    bands, rows = 2 * majors, part * ROW_CHUNKS
    wanted = (major * 2 + minor) ^ (2 * pl.program_id(0) + base)
    tile_row = (wanted * lanes + lane) * rows // tile

    @pl.when(pl.program_id(0) == 0)
    def _():
        wanted_rows = [
            (((major * 2 + minor) ^ (2 * i + base)) * lanes + lane) * rows // tile for i in range(out_calls)
        ]
        used = [
            (column_ref[row * sum(groups) + slot], slot < count_ref[row])
            for row in wanted_rows
            for slot in range(sum(groups))
        ]
        copies = []
        for i in range(2 * lanes):
            turn, flip = i // 2, i % 2
            for key in range(majors):
                alpha = (((band // 2) ^ key) * 2 + (minor ^ flip)) * lanes + lax.rem(lane + lanes - turn, lanes)
                column = alpha * rows // tile
                needed = functools.reduce(jnp.logical_or, [(one == column) & filled for one, filled in used])
                for number in range(i, len(parts), 2 * lanes):
                    first = pl.multiple_of(alpha * rows + number // (2 * lanes) * part, part)
                    target = coeff_ref.at[pl.ds(first, part)]
                    source = parts[number].at[key]
                    copies.append((needed, pltpu.make_async_copy(source, target, sems.at[number * majors + key])))
        for needed, copy in copies:
            pl.when(needed)(copy.start)
        for needed, copy in copies:
            pl.when(needed)(copy.wait)

    def product(number, i, slot):
        first = pl.multiple_of(column_ref[tile_row * sum(groups) + slot] * tile, tile)
        left = [couplings[number * pieces + piece][0, i, :chunk] for piece in range(pieces)]
        left = jnp.concatenate(left, axis=0)
        return jnp.dot(left, coeff_ref[pl.ds(first, tile), :], preferred_element_type=jnp.float32) * scale_ref[0]

    def store(value, add):
        for piece in range(pieces):
            first = (major ^ piece) * chunk if pieces > 1 else 0
            place = pl.ds(pl.multiple_of(first, chunk), chunk)
            rows_of = value[piece * chunk : (piece + 1) * chunk]
            out_ref[0, place, :] = out_ref[0, place, :] + rows_of if add else rows_of

    slot = 0
    for number, count in enumerate(groups):
        for i in range(count):
            if slot == 0:
                store(product(number, i, slot), False)
            else:
                pl.when(slot < count_ref[tile_row])(lambda: store(product(number, i, slot), True))
            slot += 1

    mirror_ref[0] = out_ref[0].T


def products(grid, couplings, parts, ids, entries, tile_cols, tile_count, scale, base):
    bands, lanes = grid.bands, grid.lanes
    groups, pieces = [group[0].shape[1] for group in couplings], len(couplings[0])
    tile = couplings[0][0].shape[3]
    majors, part, strip = parts[0].shape
    rows = part * ROW_CHUNKS // 2
    chunk = rows // pieces

    def spec(count):
        def block(i, ids, entries, *_):
            wanted = (ids[2] * 2 + ids[3]) ^ (2 * i + base)
            return (entries[ids[0] * bands + wanted], 0, 0, 0)

        return pl.BlockSpec((1, count, chunk, tile), block)

    calls = bands // 2
    return pl.pallas_call(
        lambda *refs: product_kernel(groups, pieces, lanes, calls, base, *refs),
        grid_spec=pltpu.PrefetchScalarGridSpec(
            num_scalar_prefetch=5,
            grid=(calls,),
            in_specs=[spec(count) for count in groups for _ in range(pieces)]
            + [pl.BlockSpec(memory_space=pltpu.HBM)] * len(parts),
            out_specs=[
                pl.BlockSpec((1, rows, strip), lambda i, *_: (i, 0, 0)),
                pl.BlockSpec((1, strip, rows), lambda i, *_: (i, 0, 0)),
            ],
            scratch_shapes=[
                pltpu.VMEM((len(parts) * majors * part, strip), jnp.bfloat16),
                pltpu.SemaphoreType.DMA((len(parts) * majors,)),
            ],
        ),
        out_shape=[
            jax.ShapeDtypeStruct((calls, rows, strip), jnp.float32),
            jax.ShapeDtypeStruct((calls, strip, rows), jnp.float32),
        ],
        compiler_params=pltpu.CompilerParams(vmem_limit_bytes=32 << 20),
        cost_estimate=pl.CostEstimate(
            flops=2 * calls * sum(groups) * rows * tile * strip,
            bytes_accessed=2 * (calls * sum(groups) * rows * tile + len(parts) * majors * part * strip),
            transcendentals=0,
        ),
    )(
        ids,
        entries,
        tile_cols.reshape(-1),
        tile_count,
        scale[None],
        *[piece for group in couplings for piece in group],
        *parts,
    )


def bring_home(grid, run, ids, band, lane, major, minor):
    bands, lanes, majors = grid.bands, grid.lanes, grid.majors
    received, table, gate, arrivals = [None] * bands, {}, [], []
    for base in range(2):
        sigma, mirrored = run(after(ids, gate), base)
        strip, part = mirrored.shape[1:]
        share = strip // lanes
        sigma, mirrored = sigma.astype(jnp.float16), mirrored.astype(jnp.float16)
        gate = [sigma, mirrored]
        if base:
            sigma, mirrored = after((sigma, mirrored), arrivals)
        for i in range(majors):
            key = 2 * i + base
            received[key] = grid.send(
                sigma[i],
                lambda z, x, m, n: ((m * 2 + n) ^ key, x, z // 2, z % 2),
                lambda z, x, m, n: (z, (x + 1) % lanes, m, n),
                None if base else arrivals,
            )
            for turn in range(lanes):
                piece = lax.dynamic_slice_in_dim(mirrored[i], (lane ^ turn) * share, share, 0)
                table[key, turn] = grid.send(piece, lambda z, x, m, n: (z, x ^ turn, m ^ i, n ^ base))

    rows = 2 * part
    direct = jnp.zeros((rows, lanes * rows), jnp.float16)
    for key in range(majors):
        pair = jnp.concatenate(ordered(received[2 * key : 2 * key + 2], band % 2))
        for x in range(lanes):
            first = (x * majors + ((band // 2) ^ key)) * share
            direct = lax.dynamic_update_slice_in_dim(direct, pair[:, x * share : (x + 1) * share], first, 1)
    mirror = jnp.zeros((rows, lanes * rows), jnp.float16)
    for turn in range(lanes):
        for flip in range(2):
            block = jnp.concatenate(ordered([table[2 * key + flip, turn] for key in range(majors)], major))
            first = ((lane ^ turn) * 2 + (minor ^ flip)) * part
            mirror = lax.dynamic_update_slice_in_dim(mirror, block, first, 1)
    return direct, mirror


def body(coeffs, denominator, coupling, tile_cols, tile_count):
    rows = coeffs.shape[0]
    _, slots, tile = coupling.shape
    grid = Grid(lax.axis_size("alpha"), lax.axis_size("beta"))
    alpha, beta = lax.axis_index("alpha"), lax.axis_index("beta")
    band, lane = alpha // grid.lanes, alpha % grid.lanes
    major, minor = beta // 2, beta % 2
    ids = jnp.stack([band, lane, major, minor]).astype(jnp.int32)
    all_rows = (jnp.arange(grid.bands * grid.lanes) * rows // tile).reshape(grid.bands, grid.lanes)
    many = tile_count[all_rows] > slots // 2
    busy = jnp.take(many, lane, axis=1)

    def one_busy(*values):
        return spread_inputs(grid, *values, busy, band, lane, major, minor)

    def any_busy(*values):
        return spread_inputs(grid, *values, None, band, lane, major, minor)

    couplings, largest, parts = lax.cond(
        jnp.max(jnp.sum(many, axis=0)) <= 1, one_busy, any_busy, coupling, coeffs
    )
    entries = jnp.array([row.index(z) for row in line_order(grid.bands) for z in range(grid.bands)], jnp.int32)
    growth = slots * tile * COUPLING_MAX
    current = coeffs
    for step_index in range(STEPS):
        scale = HALF_TOP / (growth * largest)
        largest = largest * (1 + 2 * growth / DENOMINATOR_MIN)
        if step_index:
            half = current.astype(jnp.bfloat16)
            parts = to_columns(grid, half, band, lane, major, minor, [], [ROW_CHUNKS // 2] * 2, False)

        def run(ids, base):
            return products(grid, couplings, parts, ids, entries, tile_cols, tile_count, scale, base)

        direct, mirror = bring_home(grid, run, ids, band, lane, major, minor)
        total = (direct.astype(jnp.float32) + mirror.astype(jnp.float32)) / scale
        current = current - total / denominator
    return current


def solution(mesh):
    placed = (P("alpha", "beta"), P("alpha", "beta"), P("alpha", None, None), P(), P())
    return jax.shard_map(
        body, mesh=mesh, in_specs=placed, out_specs=P("alpha", "beta"), check_vma=False
    )
```

```python
import functools

import jax
import jax.numpy as jnp
from jax import lax
from jax.experimental import pallas as pl
from jax.experimental.pallas import tpu as pltpu
from jax.sharding import PartitionSpec as P

STEPS = 2
COUPLING_MAX = 0.15625
DENOMINATOR_MIN = 1.5
HALF_TOP = 60000.0
AXES = ("alpha", "beta")
ROW_CHUNKS = 4


class Grid:
    def __init__(self, alpha_devices, beta_devices):
        self.bands = beta_devices
        self.lanes = alpha_devices // beta_devices
        self.majors = beta_devices // 2
        self.places = [
            (band, lane, major, minor)
            for band in range(self.bands)
            for lane in range(self.lanes)
            for major in range(self.majors)
            for minor in range(2)
        ]

    def index(self, band, lane, major, minor):
        return ((band * self.lanes + lane) * self.majors + major) * 2 + minor

    def send(self, value, where, idle=None, arrivals=None):
        stays = [where(*place) == place for place in self.places]
        if all(stays):
            return value
        pairs = []
        for place, stay in zip(self.places, stays):
            target = idle(*place) if stay else where(*place)
            pairs.append((self.index(*place), self.index(*target)))
        received = lax.ppermute(value, AXES, pairs)
        if arrivals is not None:
            arrivals.append(received)
        if any(stays):
            device = lax.axis_index("alpha") * self.bands + lax.axis_index("beta")
            received = jnp.where(jnp.array(stays)[device], value, received)
        return received


def after(value, *earlier):
    earlier = jax.tree.leaves(earlier)
    return lax.optimization_barrier((value, *earlier))[0] if earlier else value


def bits(count):
    return [1 << i for i in reversed(range(count.bit_length() - 1))]


def ordered(entries, me):
    if len(entries) == 1:
        return entries
    half = len(entries) // 2
    near, far = ordered(entries[:half], me), ordered(entries[half:], me)
    low = (me & half) == 0
    pairs = list(zip(near, far))
    return [jnp.where(low, a, b) for a, b in pairs] + [jnp.where(low, b, a) for a, b in pairs]


def line_order(bands):
    order, half = [[z] for z in range(bands)], 1
    while half < bands:
        middle = [z // (2 * half) * 2 * half + half - (z // half % 2) for z in range(bands)]
        order, half = [order[z] + order[middle[z]] for z in range(bands)], 2 * half
    return order


def gather_bands(grid, own, band, busy=None):
    held = own[None]
    brought = []
    width = 2
    while width <= grid.bands:
        half = width // 2
        moving, kept = held, None
        for hop in range(half):
            partner = list(range(grid.bands))
            for base in range(0, grid.bands, width):
                low, high = base + half - 1, base + half
                if hop == 0:
                    pairs = [(low, high)]
                else:
                    pairs = [(low - hop + 1, low - hop), (high + hop - 1, high + hop)]
                for one, other in pairs:
                    partner[one], partner[other] = other, one
            pairs = [
                (grid.index(z, x, m, n), grid.index(partner[z], x, m, 1 - n if partner[z] == z else n))
                for z, x, m, n in grid.places
            ]
            moving = lax.ppermute(moving, AXES, pairs)
            if hop == 0:
                brought.append(moving)
            takes = [(half - 1 - z % width if z % width < half else z % width - half) == hop for z in range(grid.bands)]
            kept = moving if kept is None else jnp.where(jnp.array(takes)[band], moving, kept)
        if busy is None:
            held = jnp.concatenate([held, kept])
        else:
            mine = jnp.any(busy & (jnp.arange(grid.bands) // half == band // half))
            held = jnp.where(mine, held, kept)
        width *= 2
    return held, brought


def spread_majors(grid, line):
    pieces = {0: line}
    for bit in bits(grid.majors):
        received = {key ^ bit: grid.send(piece, lambda z, x, m, n: (z, x, m ^ bit, n)) for key, piece in pieces.items()}
        pieces.update(received)
    return [pieces[key] for key in range(grid.majors)]


def spread_inputs(grid, coupling, coeffs, busy, band, lane, major, minor):
    rows, slots, tile = coupling.shape
    chunk = rows // (2 * grid.majors)
    first = (minor * grid.majors + major) * chunk
    dense = slots if busy is None else slots // 2
    groups = [(slot, 1) for slot in range(dense)]
    if busy is not None:
        groups.append((dense, slots - dense))
    rider = 1
    lines, gates = [], [None]
    half, extreme = None, None
    for number, (slot, count) in enumerate(groups):
        source = after(coupling, gates[-1])
        own = [lax.dynamic_slice(source, (first, slot + i, 0), (chunk, 1, tile)) for i in range(count)]
        own = jnp.concatenate([one.reshape(1, chunk, tile) for one in own])
        if number == 0:
            half = after(coeffs, own).astype(jnp.bfloat16)
            extreme = jnp.max(jnp.abs(lax.optimization_barrier(half))).astype(jnp.float32)
            extreme = (jnp.maximum(extreme, 1e-30) * 1.01).astype(jnp.bfloat16)
            extreme = jnp.full((16, tile), extreme)
        if number == rider:
            for where in (lambda z, x, m, n: (z, x, m, 1 - n), lambda z, x, m, n: (z, (x + 1) % grid.lanes, m, n)):
                extreme = jnp.maximum(extreme, grid.send(extreme, where))
            own = jnp.concatenate([own, jnp.broadcast_to(extreme, (count, *extreme.shape))], axis=1)
        line, brought = gather_bands(grid, own, band, None if slot < dense else busy)
        gates.append(brought[0])
        lines.append((line, brought))
    gathered = [spread_majors(grid, line) for line, _ in lines]
    rode = [piece[:, 0, chunk, 0] for piece in gathered[rider]]
    largest = jnp.max(jnp.stack(rode)).astype(jnp.float32)
    z_gates = [lines[0][0], lines[1][1][-1], gathered[0][-1], gathered[1][-1]]
    parts = to_columns(grid, half, band, lane, major, minor, z_gates, [ROW_CHUNKS], True)
    result = []
    for (slot, count), pieces in zip(groups, gathered):
        if slot >= dense:
            pieces = [jnp.broadcast_to(piece, (grid.bands, *piece.shape[1:])) for piece in pieces]
        if chunk % 16:
            whole = jnp.take(jnp.stack(pieces), major ^ jnp.arange(grid.majors), axis=0)[:, :, :, :chunk]
            pieces = [whole.transpose(1, 2, 0, 3, 4).reshape(grid.bands, count, rows // 2, tile)]
        result.append(pieces)
    if busy is None:
        late, result = result[dense // 2 :], result[: dense // 2]
        kept = rows // 2 // len(late[0])
        joined = [jnp.concatenate([one[:, :, :kept] for one in ones], axis=1) for ones in zip(*late)]
        result.append(joined)
    return result, largest, parts


def to_columns(grid, half, band, lane, major, minor, gates, batches, by_lane):
    rows = half.shape[0]
    lanes, majors = grid.lanes, grid.majors
    part, share = rows // ROW_CHUNKS, rows // majors

    def idle(z, x, m, n):
        return (z, (x + 1) % lanes, m, n) if by_lane else (z, x, m ^ 1, n)

    firsts, done = [], 0
    for batch in batches:
        block = half[done * part : (done + batch) * part]
        first = []
        for key in range(majors):
            piece = [
                lax.dynamic_slice_in_dim(block, (x * majors + (major ^ key)) * share, share, 1) for x in range(lanes)
            ]
            first.append(grid.send(jnp.concatenate(piece, 1), lambda z, x, m, n: (z, x, m ^ key, n)))
        firsts += [[one[i * part : (i + 1) * part] for one in first] for i in range(batch)]
        done += batch
    parts, earlier = [], [None] * majors
    for chunk, first in enumerate(firsts):
        first = jnp.stack(first)
        second = []
        for key in range(majors):
            piece = lax.dynamic_index_in_dim(first, (band // 2) ^ key ^ major, 0, keepdims=False)
            piece = after(piece, earlier[key], gates[min(chunk, len(gates) - 1)] if gates else None)
            piece = grid.send(piece, lambda z, x, m, n: ((z // 2 ^ key) * 2 + n, x, m, z % 2), idle)
            earlier[key] = piece
            second.append(piece)
        second = jnp.stack(second)
        for turn in range(lanes):
            third = grid.send(second, lambda z, x, m, n: (z, (x + turn) % lanes, m, n))
            parts += [third, grid.send(third, lambda z, x, m, n: (z, x, m, 1 - n))]
    return parts


def product_kernel(groups, pieces, lanes, out_calls, base, id_ref, entry_ref, column_ref, count_ref, scale_ref, *refs):
    couplings, parts = refs[: len(groups) * pieces], refs[len(groups) * pieces : -4]
    out_ref, mirror_ref, coeff_ref, sems = refs[-4:]
    band, lane, major, minor = (id_ref[i] for i in range(4))
    chunk = out_ref.shape[1] // pieces
    tile = couplings[0].shape[3]
    majors, part, _ = parts[0].shape
    bands, rows = 2 * majors, part * ROW_CHUNKS
    wanted = (major * 2 + minor) ^ (2 * pl.program_id(0) + base)
    tile_row = (wanted * lanes + lane) * rows // tile

    @pl.when(pl.program_id(0) == 0)
    def _():
        wanted_rows = [
            (((major * 2 + minor) ^ (2 * i + base)) * lanes + lane) * rows // tile for i in range(out_calls)
        ]
        used = [
            (column_ref[row * sum(groups) + slot], slot < count_ref[row])
            for row in wanted_rows
            for slot in range(sum(groups))
        ]
        copies = []
        for i in range(2 * lanes):
            turn, flip = i // 2, i % 2
            for key in range(majors):
                alpha = (((band // 2) ^ key) * 2 + (minor ^ flip)) * lanes + lax.rem(lane + lanes - turn, lanes)
                column = alpha * rows // tile
                needed = functools.reduce(jnp.logical_or, [(one == column) & filled for one, filled in used])
                for number in range(i, len(parts), 2 * lanes):
                    first = pl.multiple_of(alpha * rows + number // (2 * lanes) * part, part)
                    target = coeff_ref.at[pl.ds(first, part)]
                    source = parts[number].at[key]
                    copies.append((needed, pltpu.make_async_copy(source, target, sems.at[number * majors + key])))
        for needed, copy in copies:
            pl.when(needed)(copy.start)
        for needed, copy in copies:
            pl.when(needed)(copy.wait)

    def product(number, i, slot):
        first = pl.multiple_of(column_ref[tile_row * sum(groups) + slot] * tile, tile)
        left = [couplings[number * pieces + piece][0, i, :chunk] for piece in range(pieces)]
        left = jnp.concatenate(left, axis=0)
        return jnp.dot(left, coeff_ref[pl.ds(first, tile), :], preferred_element_type=jnp.float32) * scale_ref[0]

    def store(value, add):
        for piece in range(pieces):
            first = (major ^ piece) * chunk if pieces > 1 else 0
            place = pl.ds(pl.multiple_of(first, chunk), chunk)
            rows_of = value[piece * chunk : (piece + 1) * chunk]
            out_ref[0, place, :] = out_ref[0, place, :] + rows_of if add else rows_of

    slot = 0
    for number, count in enumerate(groups):
        for i in range(count):
            if slot == 0:
                store(product(number, i, slot), False)
            else:
                pl.when(slot < count_ref[tile_row])(lambda: store(product(number, i, slot), True))
            slot += 1

    mirror_ref[0] = out_ref[0].T


def products(grid, couplings, parts, ids, entries, tile_cols, tile_count, scale, base):
    bands, lanes = grid.bands, grid.lanes
    groups, pieces = [group[0].shape[1] for group in couplings], len(couplings[0])
    tile = couplings[0][0].shape[3]
    majors, part, strip = parts[0].shape
    rows = part * ROW_CHUNKS // 2
    chunk = rows // pieces

    def spec(count):
        def block(i, ids, entries, *_):
            wanted = (ids[2] * 2 + ids[3]) ^ (2 * i + base)
            return (entries[ids[0] * bands + wanted], 0, 0, 0)

        return pl.BlockSpec((1, count, chunk, tile), block)

    calls = bands // 2
    return pl.pallas_call(
        lambda *refs: product_kernel(groups, pieces, lanes, calls, base, *refs),
        grid_spec=pltpu.PrefetchScalarGridSpec(
            num_scalar_prefetch=5,
            grid=(calls,),
            in_specs=[spec(count) for count in groups for _ in range(pieces)]
            + [pl.BlockSpec(memory_space=pltpu.HBM)] * len(parts),
            out_specs=[
                pl.BlockSpec((1, rows, strip), lambda i, *_: (i, 0, 0)),
                pl.BlockSpec((1, strip, rows), lambda i, *_: (i, 0, 0)),
            ],
            scratch_shapes=[
                pltpu.VMEM((len(parts) * majors * part, strip), jnp.bfloat16),
                pltpu.SemaphoreType.DMA((len(parts) * majors,)),
            ],
        ),
        out_shape=[
            jax.ShapeDtypeStruct((calls, rows, strip), jnp.float32),
            jax.ShapeDtypeStruct((calls, strip, rows), jnp.float32),
        ],
        compiler_params=pltpu.CompilerParams(vmem_limit_bytes=32 << 20),
        cost_estimate=pl.CostEstimate(
            flops=2 * calls * sum(groups) * rows * tile * strip,
            bytes_accessed=2 * (calls * sum(groups) * rows * tile + len(parts) * majors * part * strip),
            transcendentals=0,
        ),
    )(
        ids,
        entries,
        tile_cols.reshape(-1),
        tile_count,
        scale[None],
        *[piece for group in couplings for piece in group],
        *parts,
    )


def bring_home(grid, run, ids, band, lane, major, minor):
    bands, lanes, majors = grid.bands, grid.lanes, grid.majors
    received, table, gate, arrivals = [None] * bands, {}, [], []
    for base in range(2):
        sigma, mirrored = run(after(ids, gate), base)
        strip, part = mirrored.shape[1:]
        share = strip // lanes
        sigma, mirrored = sigma.astype(jnp.float16), mirrored.astype(jnp.float16)
        gate = [sigma, mirrored]
        if base:
            sigma, mirrored = after((sigma, mirrored), arrivals)
        for i in range(majors):
            key = 2 * i + base
            received[key] = grid.send(
                sigma[i],
                lambda z, x, m, n: ((m * 2 + n) ^ key, x, z // 2, z % 2),
                lambda z, x, m, n: (z, (x + 1) % lanes, m, n),
                None if base else arrivals,
            )
            for turn in range(lanes):
                piece = lax.dynamic_slice_in_dim(mirrored[i], (lane ^ turn) * share, share, 0)
                table[key, turn] = grid.send(piece, lambda z, x, m, n: (z, x ^ turn, m ^ i, n ^ base))

    rows = 2 * part
    direct = jnp.zeros((rows, lanes * rows), jnp.float16)
    for key in range(majors):
        pair = jnp.concatenate(ordered(received[2 * key : 2 * key + 2], band % 2))
        for x in range(lanes):
            first = (x * majors + ((band // 2) ^ key)) * share
            direct = lax.dynamic_update_slice_in_dim(direct, pair[:, x * share : (x + 1) * share], first, 1)
    mirror = jnp.zeros((rows, lanes * rows), jnp.float16)
    for turn in range(lanes):
        for flip in range(2):
            block = jnp.concatenate(ordered([table[2 * key + flip, turn] for key in range(majors)], major))
            first = ((lane ^ turn) * 2 + (minor ^ flip)) * part
            mirror = lax.dynamic_update_slice_in_dim(mirror, block, first, 1)
    return direct, mirror


def body(coeffs, denominator, coupling, tile_cols, tile_count):
    rows = coeffs.shape[0]
    _, slots, tile = coupling.shape
    grid = Grid(lax.axis_size("alpha"), lax.axis_size("beta"))
    alpha, beta = lax.axis_index("alpha"), lax.axis_index("beta")
    band, lane = alpha // grid.lanes, alpha % grid.lanes
    major, minor = beta // 2, beta % 2
    ids = jnp.stack([band, lane, major, minor]).astype(jnp.int32)
    many = jnp.repeat(tile_count, tile // rows).reshape(grid.bands, grid.lanes) > slots // 2
    busy = lax.dynamic_index_in_dim(many, lane, 1, keepdims=False)

    def one_busy(*values):
        return spread_inputs(grid, *values, busy, band, lane, major, minor)

    def any_busy(*values):
        return spread_inputs(grid, *values, None, band, lane, major, minor)

    couplings, largest, parts = lax.cond(
        jnp.max(jnp.sum(many, axis=0)) <= 1, one_busy, any_busy, coupling, coeffs
    )
    entries = jnp.array([row.index(z) for row in line_order(grid.bands) for z in range(grid.bands)], jnp.int32)
    growth = slots * tile * COUPLING_MAX
    current = coeffs
    for step_index in range(STEPS):
        scale = HALF_TOP / (growth * largest)
        largest = largest * (1 + 2 * growth / DENOMINATOR_MIN)
        if step_index:
            half = current.astype(jnp.bfloat16)
            parts = to_columns(grid, half, band, lane, major, minor, [], [ROW_CHUNKS // 2] * 2, False)

        def run(ids, base):
            return products(grid, couplings, parts, ids, entries, tile_cols, tile_count, scale, base)

        direct, mirror = bring_home(grid, run, ids, band, lane, major, minor)
        total = (direct.astype(jnp.float32) + mirror.astype(jnp.float32)) / scale
        current = current - total / denominator
    return current


def solution(mesh):
    placed = (P("alpha", "beta"), P("alpha", "beta"), P("alpha", None, None), P(), P())
    return jax.shard_map(
        body, mesh=mesh, in_specs=placed, out_specs=P("alpha", "beta"), check_vma=False
    )
```
